512 devices in a mesh: lon: 32 (over x_lo, z), lat: 16 (over y, x_hi, core).
Axes of the slice: x: 4 (x_hi: 2, x_lo: 2; x = x_hi * 2 + x_lo), y: 4, z: 16, core: 2. Of those that a mesh axis runs over, the one named last changes fastest.
Arguments:
- heat_state: float32 [64, 128, 8192], P(None, 'lat', 'lon'), may hold values from -6 to 6
- salt_anomaly: float32 [64, 128, 8192], P(None, 'lat', 'lon'), may hold values from -6 to 6
- zonal_current: float32 [64, 128, 8192], P(None, 'lat', 'lon'), may hold values from -4 to 4
- meridional_current: float32 [64, 128, 8192], P(None, 'lat', 'lon'), may hold values from -4 to 4
- ocean_layer_number: int32 [128, 8192], P('lat', 'lon'), may hold values from 0 to 64, as said below
- sea_elevation: float32 [128, 8192], P('lat', 'lon'), may hold values from -6 to 6
- zonal_mean_current: float32 [128, 8192], P('lat', 'lon'), may hold values from -3 to 3
- meridional_mean_current: float32 [128, 8192], P('lat', 'lon'), may hold values from -3 to 3
- first_layer_matrix: bfloat16 [128, 256], replicated, may hold values from -0.5 to 0.5
- second_layer_matrix: bfloat16 [256, 64], replicated, may hold values from -0.375 to 0.375
Outputs:
- next_heat_state: float32 [64, 128, 8192], P(None, 'lat', 'lon')
- next_salt_anomaly: float32 [64, 128, 8192], P(None, 'lat', 'lon')
- height_next: float32 [128, 8192], P('lat', 'lon')
- east_next: float32 [128, 8192], P('lat', 'lon')
- north_next: float32 [128, 8192], P('lat', 'lon')
The draws below stay inside these ranges and needn't reach their ends.
Inputs may be any that keep to these rules, and one draw needn't show every extreme that they name: `ocean_layer_number`: tiles of 8 rows by 32 columns, aligned, are, except the tile holding row 0 and column 0, either all land (no wet levels) or ocean with independent depths; some columns are fully deep and some are land.
All inputs are finite; a program needn't handle non-finite values.
Results may differ from the reference program's by a relative error of at most 0.0003.
Values sent between devices are 32-bit elements; how exact they have to be, the bound alone decides.
A program may use at most 64 MiB of HBM per device.

```python
import math
import jax
import jax.numpy as jnp
from jax import lax

LAYER_NUMBER = 64
HID = 256
SUBSTEPS = 4
PARALLEL_SHARE = 8
PARALLEL_ALL = 128
MERIDIAN_ALL = 8192


def draw_ocean_layer_number(key, part):
    key = jax.random.fold_in(key, 11)
    depth_key, tile_key = jax.random.split(key)
    depths = jax.random.randint(depth_key, (PARALLEL_ALL, MERIDIAN_ALL), 0, LAYER_NUMBER + 1)
    tiles = jax.random.randint(tile_key, (PARALLEL_ALL // 8, MERIDIAN_ALL // 32), 0, 4)
    land = jnp.repeat(jnp.repeat(tiles == 0, 8, axis=0), 32, axis=1)
    levels = jnp.where(land, 0, depths)
    levels = levels.at[0, 0].set(LAYER_NUMBER)
    levels = levels.at[PARALLEL_ALL - 1, MERIDIAN_ALL - 1].set(0)
    return levels.astype(jnp.int32)


def level_of(stream_key, extent, shards, low, largest):
    level, own = 1.0, jax.random.fold_in(stream_key, 6)
    for dim, blocks in shards:
        draws = jnp.exp(jax.random.uniform(jax.random.fold_in(own, dim), (blocks,), jnp.float32, low / len(shards), largest / len(shards)))
        level = level * jnp.repeat(draws, extent[dim] // blocks).reshape([-1 if axis == dim else 1 for axis in range(len(extent))])
    return level


def normal_values(own_key, extent, deviation, most, shards=(), held_as=jnp.bfloat16):
    gain = level_of(own_key, extent, shards, -0.22, 0.18) if shards else 1.0
    array = jax.random.normal(own_key, extent, jnp.float32) * deviation * gain
    return jnp.minimum(jnp.maximum(array, -most), most).astype(held_as)


def setup_inputs(seed: int = 0) -> dict:
    keys = jax.random.split(jax.random.key(seed), 11)
    return {
        "heat_state": normal_values(keys[0], (LAYER_NUMBER, PARALLEL_ALL, MERIDIAN_ALL), 1.0, 6.0, ((1, 16), (2, 32)), jnp.float32),
        "salt_anomaly": normal_values(keys[1], (LAYER_NUMBER, PARALLEL_ALL, MERIDIAN_ALL), 1.0, 6.0, ((1, 16), (2, 32)), jnp.float32),
        "zonal_current": normal_values(keys[2], (LAYER_NUMBER, PARALLEL_ALL, MERIDIAN_ALL), 1.0, 4.0, ((1, 16), (2, 32)), jnp.float32),
        "meridional_current": normal_values(keys[3], (LAYER_NUMBER, PARALLEL_ALL, MERIDIAN_ALL), 1.0, 4.0, ((1, 16), (2, 32)), jnp.float32),
        "ocean_layer_number": draw_ocean_layer_number(jax.random.fold_in(keys[10], 71), 0),
        "sea_elevation": normal_values(keys[5], (PARALLEL_ALL, MERIDIAN_ALL), 1.0, 6.0, ((0, 16), (1, 32)), jnp.float32),
        "zonal_mean_current": normal_values(keys[6], (PARALLEL_ALL, MERIDIAN_ALL), 0.5, 3.0, ((0, 16), (1, 32)), jnp.float32),
        "meridional_mean_current": normal_values(keys[7], (PARALLEL_ALL, MERIDIAN_ALL), 0.5, 3.0, ((0, 16), (1, 32)), jnp.float32),
        "first_layer_matrix": normal_values(keys[8], (2 * LAYER_NUMBER, HID), (2 * LAYER_NUMBER) ** -0.5, 0.5),
        "second_layer_matrix": normal_values(keys[9], (HID, LAYER_NUMBER), HID ** -0.5, 0.375),
    }


ADVECT = 0.1
SMOOTHING = 0.1
GRAVITY = 0.3
SPREADING = 0.3
BUOYANCY = 0.5
THERMAL = 0.2
HALINE = 0.15
MIXING_MAX = 0.45

def level_mask(seafloor_matrix, layer_number):
    level_axis = lax.broadcasted_iota(jnp.float32, (layer_number,) + seafloor_matrix.shape, 0)
    return (level_axis < seafloor_matrix[None]).astype(jnp.float32)

def face_flux(lower, upper, speed_lower, speed_upper, shared):
    return shared * (ADVECT * 0.25 * (speed_lower + speed_upper) * (lower + upper) - SMOOTHING * (upper - lower))

def sideways_share(tracer, zonal_flow_rate, meridional_rate, ocean_layer_flags):
    centre = tracer[:, 1:-1, 1:-1]
    interior_slice = ocean_layer_flags[:, 1:-1, 1:-1]
    east_face = face_flux(centre, tracer[:, 1:-1, 2:], zonal_flow_rate[:, 1:-1, 1:-1], zonal_flow_rate[:, 1:-1, 2:], interior_slice * ocean_layer_flags[:, 1:-1, 2:])
    west_face = face_flux(tracer[:, 1:-1, :-2], centre, zonal_flow_rate[:, 1:-1, :-2], zonal_flow_rate[:, 1:-1, 1:-1], ocean_layer_flags[:, 1:-1, :-2] * interior_slice)
    north_face = face_flux(centre, tracer[:, 2:, 1:-1], meridional_rate[:, 1:-1, 1:-1], meridional_rate[:, 2:, 1:-1], interior_slice * ocean_layer_flags[:, 2:, 1:-1])
    south_face = face_flux(tracer[:, :-2, 1:-1], centre, meridional_rate[:, :-2, 1:-1], meridional_rate[:, 1:-1, 1:-1], ocean_layer_flags[:, :-2, 1:-1] * interior_slice)
    return centre - interior_slice * (east_face - west_face + north_face - south_face)

def upright_share(tracer, diffusivity_factor):
    vertical_flux = diffusivity_factor[:-1] * (tracer[1:] - tracer[:-1])
    zero_layer = jnp.zeros_like(tracer[:1])
    return tracer + jnp.concatenate([vertical_flux, zero_layer], 0) - jnp.concatenate([zero_layer, vertical_flux], 0)

def contract(weight, inputs):
    return lax.dot_general(weight, inputs, (((0,), (0,)), ((), ())), preferred_element_type=jnp.float32)

def vertical_change(bordered_matrix, first_layer_matrix, second_layer_matrix):
    layer_number = (bordered_matrix.shape[0] - 1) // 4
    heat_state = bordered_matrix[:layer_number]
    salt_anomaly = bordered_matrix[layer_number:2 * layer_number]
    zonal_flow_rate = bordered_matrix[2 * layer_number:3 * layer_number]
    meridional_rate = bordered_matrix[3 * layer_number:4 * layer_number]
    ocean_layer_flags = level_mask(bordered_matrix[4 * layer_number], layer_number)
    thermal_border = sideways_share(heat_state, zonal_flow_rate, meridional_rate, ocean_layer_flags)
    brine_neighbour = sideways_share(salt_anomaly, zonal_flow_rate, meridional_rate, ocean_layer_flags)
    interior_slice = ocean_layer_flags[:, 1:-1, 1:-1]
    row_count = interior_slice.shape[1]
    column_count = interior_slice.shape[2]
    network_entries = jnp.concatenate([thermal_border * interior_slice, brine_neighbour * interior_slice], 0)
    network_entries = network_entries.reshape(2 * layer_number, row_count * column_count).astype(jnp.bfloat16)
    hidden = jnp.tanh(contract(first_layer_matrix, network_entries)).astype(jnp.bfloat16)
    logits = contract(second_layer_matrix, hidden).reshape(layer_number, row_count, column_count)
    below = jnp.concatenate([interior_slice[1:], jnp.zeros_like(interior_slice[:1])], 0)
    diffusivity_factor = MIXING_MAX * jax.nn.sigmoid(logits) * interior_slice * below
    return (upright_share(thermal_border, diffusivity_factor), upright_share(brine_neighbour, diffusivity_factor))

def buoyancy_of(bordered_matrix):
    layer_number = (bordered_matrix.shape[0] - 1) // 4
    ocean_layer_flags = level_mask(bordered_matrix[4 * layer_number], layer_number)
    density = THERMAL * bordered_matrix[:layer_number] - HALINE * bordered_matrix[layer_number:2 * layer_number]
    return lax.optimization_barrier(jnp.sum(ocean_layer_flags * density, axis=0)) * (1.0 / math.sqrt(layer_number))

def forcing(buoyancy):
    east_force = -BUOYANCY * 0.5 * (buoyancy[1:-1, 2:] - buoyancy[1:-1, :-2])
    north_force = -BUOYANCY * 0.5 * (buoyancy[2:, 1:-1] - buoyancy[:-2, 1:-1])
    return (east_force, north_force)

def trimmed(field):
    return field[1:-1, 1:-1]

def substep(topmost_layer, layer_number):
    height = topmost_layer[0]
    east_flow = topmost_layer[1]
    north_flow = topmost_layer[2]
    east_force = topmost_layer[3]
    north_force = topmost_layer[4]
    seafloor_matrix = topmost_layer[5]
    wet_cells = (seafloor_matrix > 0).astype(jnp.float32)
    column_depth = seafloor_matrix / layer_number
    east_new = trimmed(wet_cells) * (trimmed(east_flow) - GRAVITY * 0.5 * (height[1:-1, 2:] - height[1:-1, :-2]) + trimmed(east_force))
    north_new = trimmed(wet_cells) * (trimmed(north_flow) - GRAVITY * 0.5 * (height[2:, 1:-1] - height[:-2, 1:-1]) + trimmed(north_force))
    east_carry = trimmed(column_depth) * east_new
    north_carry = trimmed(column_depth) * north_new
    divergence = east_carry[1:-1, 2:] - east_carry[1:-1, :-2] + north_carry[2:, 1:-1] - north_carry[:-2, 1:-1]
    height_new = trimmed(trimmed(wet_cells)) * (trimmed(trimmed(height)) - SPREADING * 0.5 * divergence)
    return jnp.stack([height_new, trimmed(east_new), trimmed(north_new), trimmed(trimmed(east_force)), trimmed(trimmed(north_force)), trimmed(trimmed(seafloor_matrix))])

def extend(field, width):
    beside_all = jnp.concatenate([field[..., -width:], field, field[..., :width]], axis=-1)
    padding = [(0, 0)] * (field.ndim - 2) + [(width, width), (0, 0)]
    return jnp.pad(beside_all, padding)

def reference(heat_state, salt_anomaly, zonal_current, meridional_current, ocean_layer_number, sea_elevation, zonal_mean_current, meridional_mean_current, first_layer_matrix, second_layer_matrix):
    seafloor_matrix = ocean_layer_number.astype(jnp.float32)
    joined_tracers = jnp.concatenate([heat_state, salt_anomaly, zonal_current, meridional_current, seafloor_matrix[None]], 0)
    padded = jnp.pad(joined_tracers, ((0, 0), (1, 1), (0, 0)))

    def single_piece(block_index):
        piece = lax.dynamic_slice_in_dim(padded, block_index * PARALLEL_SHARE, PARALLEL_SHARE + 2, 1)
        beside_all = jnp.concatenate([piece[..., -1:], piece, piece[..., :1]], -1)
        temp_new, salt_new = vertical_change(beside_all, first_layer_matrix, second_layer_matrix)
        return (temp_new, salt_new, buoyancy_of(beside_all)[1:-1, 1:-1])
    thermal_pieces, brine_pieces, buoyant_pieces = lax.map(single_piece, jnp.arange(PARALLEL_ALL // PARALLEL_SHARE, dtype=jnp.int32))
    next_heat_state = jnp.moveaxis(thermal_pieces, 0, 1).reshape(LAYER_NUMBER, PARALLEL_ALL, MERIDIAN_ALL)
    next_salt_anomaly = jnp.moveaxis(brine_pieces, 0, 1).reshape(LAYER_NUMBER, PARALLEL_ALL, MERIDIAN_ALL)
    buoyancy = buoyant_pieces.reshape(PARALLEL_ALL, MERIDIAN_ALL)
    east_force, north_force = forcing(extend(buoyancy, 1))
    topmost_layer = jnp.stack([sea_elevation, zonal_mean_current, meridional_mean_current, east_force, north_force, seafloor_matrix])
    for substep_index in range(SUBSTEPS):
        topmost_layer = substep(extend(topmost_layer, 2), LAYER_NUMBER)
    return (next_heat_state, next_salt_anomaly, topmost_layer[0], topmost_layer[1], topmost_layer[2])
```

```python
import functools

import jax
import jax.numpy as jnp
from jax import lax
from jax.experimental import pallas as pl
from jax.experimental.pallas import tpu as pltpu
from jax.sharding import PartitionSpec as P

MESH = pl.DeviceIdType.MESH
SUBSTEPS = 4
ADVECT = 0.1 * 0.25
SMOOTHING = 0.1
GRAVITY = 0.3 * 0.5
SPREADING = 0.3 * 0.5
BUOYANCY = 0.5 * 0.5
THERMAL = 0.2
HALINE = 0.15
MIXING_MAX = 0.45
LIMIT = 40 * 2**20
PERIOD = 16
LEVELS, ROWS, COLS, HID = 64, 8, 256, 256
GROUPS = LEVELS // 8
TILE = 128
U, T, S, V = range(4)
HEIGHT, EAST, NORTH, DEPTH, BUOYANT = range(5)
FIELDS = 5
E, W, N, S_, NE, SE, NW, SW = range(8)


def turn(x, shift, axis):
    return pltpu.roll(x, shift % x.shape[axis], axis)


def lanes_of(shape):
    return lax.broadcasted_iota(jnp.int32, shape, 1)


def levels_of(cols):
    return lax.broadcasted_iota(jnp.int32, (LEVELS, cols), 0).astype(jnp.float32)


def tall(block):
    return jnp.concatenate([block] * GROUPS, 0)


def network(w1_t, w2_t, thermal, saline):
    entries = jnp.concatenate([thermal, saline], 0).astype(jnp.bfloat16)
    hidden = jnp.tanh(jnp.dot(w1_t, entries, preferred_element_type=jnp.float32))
    return jnp.dot(
        w2_t, hidden.astype(jnp.bfloat16), preferred_element_type=jnp.float32
    )


def mixing(logits):
    return (0.5 * MIXING_MAX) * (1.0 + jnp.tanh(0.5 * logits))


def settle(tracer, kappa):
    flux = kappa * (turn(tracer, -1, 0) - tracer)
    return tracer + flux - turn(flux, 1, 0)


def face(lower, upper, speed, shared):
    return jnp.where(
        shared, ADVECT * speed * (lower + upper) - SMOOTHING * (upper - lower), 0.0
    )


def packed(vreg_of, slots, lane):
    where = lanes_of((8, TILE))
    halves = []
    for r in range(2):
        total = None
        for g in range(4):
            part = None
            for a in range(slots):
                for j in range(ROWS):
                    target = 32 * g + 8 * a + j
                    moved = turn(vreg_of(a, j, 2 * g + r), target - lane, 1)
                    base = jnp.zeros_like(moved) if part is None else part
                    part = jnp.where(where == target, moved, base)
            total = part if total is None else total + part
        halves.append(total)
    return jnp.concatenate(halves, 0)


def unfolded(folded):
    return jnp.concatenate([turn(folded, -32 * g, 1) for g in range(4)], 0)


def edge_flux(lower, upper):
    first = lanes_of(lower.shape) % 32 < 8
    total, both = lower + upper, lower * upper
    speed = jnp.where(first, turn(total, -16, 1), turn(total, -8, 1))
    shared = jnp.where(first, turn(both, -24, 1), turn(both, -16, 1))
    return shared * (ADVECT * speed * total - SMOOTHING * (upper - lower))


def exchange(
    nlon, nlat,
    t, s, u, v, depth, height, east, north, w1, w2,
    out_t, out_s, out_surface,
    x, side, surface, depth_int, w1_in, w1_t, w2_t, deep, deep_east, lon_out, lon_in, corner_in,
    load_sem, row_send, row_recv, send_sem, recv_sem, seam_sem, ready_sem,
):
    lon, lat = lax.axis_index("lon"), lax.axis_index("lat")
    z = lax.rem(lon, PERIOD)
    early, late, before = z == 0, z == PERIOD - 1, z == PERIOD - 2
    has_n, has_s = lat < nlat - 1, lat > 0
    sides = has_n.astype(jnp.int32) + has_s.astype(jnp.int32)
    to_east, to_west = lax.rem(lon + 1, nlon), lax.rem(lon + nlon - 1, nlon)
    device = {
        E: {"lon": to_east},
        W: {"lon": to_west},
        N: {"lat": lat + 1},
        S_: {"lat": lat - 1},
        NE: {"lon": to_east, "lat": lat + 1},
        SE: {"lon": to_east, "lat": lat - 1},
        NW: {"lon": to_west, "lat": lat + 1},
        SW: {"lon": to_west, "lat": lat - 1},
    }
    there = {E: True, W: True, N: has_n, NE: has_n, NW: has_n, S_: has_s, SE: has_s, SW: has_s}

    def signal(sem, way, also=True):
        @pl.when(jnp.logical_and(there[way], also))
        def _():
            pl.semaphore_signal(sem, inc=1, device_id=device[way], device_id_type=MESH)

    local = pltpu.make_async_copy
    plane = pl.ds(ROWS, ROWS)
    first = [local(depth, depth_int, load_sem.at[0])]
    first += [
        local(f, surface.at[k, plane], load_sem.at[1 + k])
        for k, f in enumerate((height, east, north))
    ]
    for c in first:
        c.start()

    def load_half(half):
        cut = pl.ds(half * TILE, TILE)
        for k, f in ((T, t), (S, s), (U, u)):
            for j in range(ROWS):
                local(f.at[:, j, cut], x.at[k, j + 1, :, cut], load_sem.at[4 + half]).start()

    def wait_half(half):
        whole = x.at[pl.ds(0, 3), pl.ds(1, ROWS), :, pl.ds(half * TILE, TILE)]
        local(whole, whole, load_sem.at[4 + half]).wait()

    load_half(1)

    barrier = pltpu.get_barrier_semaphore()
    signal(barrier, W)
    signal(barrier, NW)
    signal(barrier, SW)
    usual = jnp.logical_not(late)
    signal(barrier, E, usual)
    signal(barrier, N, usual)
    signal(barrier, S_, usual)
    inner = jnp.logical_and(usual, jnp.logical_not(before))
    signal(barrier, NE, inner)
    signal(barrier, SE, inner)

    load_half(0)
    for j in range(ROWS):
        local(v.at[:, j, :], x.at[V, j + 1], load_sem.at[6]).start()
    weights = [local(w1, w1_in, load_sem.at[7]), local(w2, w2_t, load_sem.at[8])]
    for c in weights:
        c.start()

    expected = jnp.where(early, 1 + 2 * sides, jnp.where(late, 2 + sides, 2 + 3 * sides))
    pl.semaphore_wait(barrier, expected)
    for way in (E, NE, SE):
        signal(seam_sem, way, late)
    for way in (NE, SE):
        signal(ready_sem, way, before)

    remote = pltpu.make_async_remote_copy

    def row_copies(way):
        source, target = (ROWS - 1, 0) if way == N else (0, ROWS + 1)
        k = way - N
        return [
            remote(f.at[:, source, :], x.at[a, target], row_send.at[3 * k + i], row_recv.at[1 - k],
                   device_id=device[way], device_id_type=MESH)
            for i, (a, f) in enumerate(((T, t), (S, s), (V, v)))
        ]

    opposite = {E: W, W: E, N: S_, S_: N, NE: SW, SW: NE, NW: SE, SE: NW}
    lon_slot = {E: 0, W: 1}
    corner_slot = {NE: 0, SE: 1, NW: 2, SW: 3}
    surface_rows = {N: pl.ds(2 * ROWS, ROWS), S_: pl.ds(0, ROWS)}
    tail = pl.ds(16, 8)

    def message(way):
        if way in lon_slot:
            src, dst = lon_out.at[lon_slot[way]], lon_in.at[lon_slot[opposite[way]]]
        elif way in corner_slot:
            src = lon_out.at[0 if way in (NE, SE) else 1, tail]
            dst = corner_in.at[corner_slot[opposite[way]]]
        else:
            src, dst = surface.at[:, plane], surface.at[:, surface_rows[opposite[way]]]
        return remote(src, dst, send_sem.at[way], recv_sem.at[opposite[way]],
                      device_id=device[way], device_id_type=MESH)

    def send(way, also=True):
        @pl.when(jnp.logical_and(there[way], also))
        def _():
            message(way).start()

    def send_rows(also):
        for way in (N, S_):

            @pl.when(jnp.logical_and(there[way], also))
            def _(way=way):
                for c in row_copies(way):
                    c.start()

    send_rows(usual)

    @pl.when(jnp.logical_not(has_s))
    def _():
        x[:, 0] = jnp.zeros((4, LEVELS, COLS), jnp.float32)
        surface[:, 0:ROWS] = jnp.zeros((FIELDS, ROWS, COLS), jnp.float32)
        corner_in[1] = jnp.zeros((8, TILE), jnp.float32)
        corner_in[3] = jnp.zeros((8, TILE), jnp.float32)

    @pl.when(jnp.logical_not(has_n))
    def _():
        x[:, ROWS + 1] = jnp.zeros((4, LEVELS, COLS), jnp.float32)
        surface[:, 2 * ROWS : 3 * ROWS] = jnp.zeros((FIELDS, ROWS, COLS), jnp.float32)
        corner_in[0] = jnp.zeros((8, TILE), jnp.float32)
        corner_in[2] = jnp.zeros((8, TILE), jnp.float32)

    for c in first:
        c.wait()
    deeps = depth_int[...].astype(jnp.float32)
    surface[DEPTH, plane] = deeps
    beside = jnp.where(lanes_of((ROWS, COLS)) == COLS - 1, 0.0, turn(deeps, -1, 1))
    beside = jnp.minimum(deeps, beside)
    for j in range(ROWS):
        deep[j + 1] = jnp.broadcast_to(deeps[j : j + 1], (8, COLS))
        deep_east[j] = jnp.broadcast_to(beside[j : j + 1], (8, COLS))

    def pack_half(half):
        cut = pl.ds(half * TILE, TILE)
        edge = TILE - 1 if half else 0
        level = lax.broadcasted_iota(jnp.int32, (8, TILE), 0).astype(jnp.float32)
        where = lanes_of((8, TILE))

        def wet(j, q):
            return level + 8.0 * q < deep[j + 1, :, cut]

        def vreg(a, j, q):
            if a == 3:
                return jnp.where(wet(j, q), 1.0, 0.0)
            return x[(T, S, U)[a], j + 1, pl.ds(8 * q, 8), cut]

        lon_out[1 - half, 0:16] = packed(vreg, 4, edge)
        for j in range(ROWS):
            total = jnp.zeros((8, TILE), jnp.float32)
            for q in range(GROUPS):
                rows = pl.ds(8 * q, 8)
                density = THERMAL * x[T, j + 1, rows, cut] - HALINE * x[S, j + 1, rows, cut]
                total = total + jnp.where(wet(j, q), density, 0.0)
            surface[BUOYANT, ROWS + j : ROWS + j + 1, cut] = (LEVELS**-0.5) * jnp.sum(total, 0, keepdims=True)
        kept = (where >= TILE - 8) if half else (where < 8)
        lon_out[1 - half, 16:24] = sum(
            turn(jnp.where(kept, surface[f, plane, cut], 0.0), 16 * f, 1)
            for f in range(FIELDS)
        )

    wait_half(1)
    pack_half(1)
    for way in (E, NE, SE):
        send(way)
    wait_half(0)
    pack_half(0)
    send(W, jnp.logical_not(early))
    middle = jnp.logical_and(usual, jnp.logical_not(early))
    send(NW, middle)
    send(SW, middle)
    send(N, usual)
    send(S_, usual)

    @pl.when(late)
    def _():
        pl.semaphore_wait(ready_sem, 2 * sides)

    send_rows(late)
    for way in (NW, SW, N, S_):
        send(way, late)

    for c in weights:
        c.wait()
    w1_t[...] = w1_in[...].astype(jnp.float32).T.astype(jnp.bfloat16)
    all_v = x.at[V, pl.ds(1, ROWS)]
    local(all_v, all_v, load_sem.at[6]).wait()

    def row(j):
        level = levels_of(COLS)
        speed = x[U, j + 1]
        speed = speed + turn(speed, -1, 1)
        here, above, below = deep[j + 1], deep[j + 2], deep[j]
        open_east = level < tall(deep_east[j])
        open_north = level < tall(jnp.minimum(here, above))
        open_south = level < tall(jnp.minimum(here, below))
        wet = level < tall(here)
        wet_below = level + 1.0 < tall(here)
        speed_north = x[V, j + 1] + x[V, j + 2]
        speed_south = x[V, j + 1] + x[V, j]

        def lateral(k):
            own = x[k, j + 1]
            flux = face(own, turn(own, -1, 1), speed, open_east)
            return own - (
                flux
                - turn(flux, 1, 1)
                + face(own, x[k, j + 2], speed_north, open_north)
                - face(x[k, j], own, speed_south, open_south)
            )

        thermal, saline = lateral(T), lateral(S)
        side[0, j] = thermal
        side[1, j] = saline
        logits = network(
            w1_t[...], w2_t[...], jnp.where(wet, thermal, 0.0), jnp.where(wet, saline, 0.0)
        )
        kappa = jnp.where(wet_below, mixing(logits), 0.0)
        out_t[j] = settle(thermal, kappa)
        out_s[j] = settle(saline, kappa)

    pl.loop(1, ROWS - 1)(row)

    @pl.when(early)
    def _():
        pl.semaphore_wait(seam_sem, 1 + sides)

    signal(ready_sem, NW, early)
    signal(ready_sem, SW, early)
    for way in (W, NW, SW):
        send(way, early)

    for way in (N, S_):

        @pl.when(there[way])
        def _(way=way):
            k = way - N
            rows = x.at[pl.ds(T, 3), ROWS + 1 if way == N else 0]
            local(rows, rows, row_recv.at[k]).wait()
            message(opposite[way]).wait_recv()

    deep[0] = jnp.broadcast_to(surface[DEPTH, ROWS - 1 : ROWS], (8, COLS))
    deep[ROWS + 1] = jnp.broadcast_to(surface[DEPTH, 2 * ROWS : 2 * ROWS + 1], (8, COLS))

    @pl.loop(0, 2)
    def _(i):
        row(i * (ROWS - 1))

    def side_pack(half):
        cut = pl.ds(half * TILE, TILE)
        return packed(
            lambda a, j, q: side[a, j, pl.ds(8 * q, 8), cut],
            2,
            TILE - 1 if half else 0,
        )

    part_east, part_west = side_pack(1), side_pack(0)

    for way in (E, W, NE, SE, NW, SW):

        @pl.when(there[way])
        def _(way=way):
            message(opposite[way]).wait_recv()

    own_east, own_west = lon_out[0, 0:16], lon_out[1, 0:16]
    from_east, from_west = lon_in[0, 0:16], lon_in[1, 0:16]
    at_east = part_east - edge_flux(own_east, from_east)
    at_west = part_west + edge_flux(from_west, own_west)
    lane16 = lanes_of((16, TILE))
    first_slot = lane16 % 32 < 8
    thermal = unfolded(jnp.where(first_slot, at_west, turn(at_east, 8, 1)))
    saline = unfolded(jnp.where(first_slot, turn(at_west, -8, 1), at_east))
    wet = unfolded(jnp.where(first_slot, turn(own_west, -24, 1), turn(own_east, -16, 1)))
    lane = lanes_of((LEVELS, TILE))
    wet = jnp.where(lane < 16, wet, 0.0)
    wet_below = jnp.where(levels_of(TILE) < LEVELS - 1.0, turn(wet, -1, 0), 0.0)
    logits = network(w1_t[...], w2_t[...], thermal * wet, saline * wet)
    kappa = mixing(logits) * wet * wet_below
    for out, tracer in ((out_t, thermal), (out_s, saline)):
        new = settle(tracer, kappa)
        for j in range(ROWS):
            out[j, :, 0:TILE] = jnp.where(lane == 0, turn(new, -j, 1), out[j, :, 0:TILE])
            out[j, :, TILE:] = jnp.where(lane == TILE - 1, turn(new, TILE - 1 - 8 - j, 1), out[j, :, TILE:])

    third = jnp.concatenate(
        [
            corner_in[1] + corner_in[3],
            lon_in[0, 16:24] + lon_in[1, 16:24],
            corner_in[0] + corner_in[2],
        ],
        0,
    )
    where = lanes_of((3 * ROWS, TILE))
    around = jnp.logical_or(where < 8, where >= TILE - 8)
    field = [
        jnp.concatenate([surface[f], jnp.where(around, turn(third, -16 * f, 1), 0.0)], 1)
        for f in range(FIELDS)
    ]
    h, e, n, d, b = field
    land = d <= 0.0
    column = d * (1.0 / LEVELS)

    def eastward(a):
        return turn(a, -1, 1) - turn(a, 1, 1)

    def northward(a):
        return turn(a, -1, 0) - turn(a, 1, 0)

    east_force, north_force = -BUOYANCY * eastward(b), -BUOYANCY * northward(b)
    for _ in range(SUBSTEPS):
        e = jnp.where(land, 0.0, e - GRAVITY * eastward(h) + east_force)
        n = jnp.where(land, 0.0, n - GRAVITY * northward(h) + north_force)
        h = jnp.where(land, 0.0, h - SPREADING * (eastward(column * e) + northward(column * n)))
    for k, a in enumerate((h, e, n)):
        out_surface[k] = a[ROWS : 2 * ROWS, 0:COLS]

    for way in (N, S_):

        @pl.when(there[way])
        def _(way=way):
            for c in row_copies(way):
                c.wait_send()

    for way in range(8):

        @pl.when(there[way])
        def _(way=way):
            message(way).wait_send()


def deliver(t, s, surface, out_t, out_s, height, east, north, sem):
    copies = []
    for src, dst in ((t, out_t), (s, out_s)):
        copies += [(src.at[j], dst.at[:, j, :]) for j in range(ROWS)]
    copies += [(surface.at[k], dst) for k, dst in enumerate((height, east, north))]
    copies = [pltpu.make_async_copy(a, b, sem.at[i]) for i, (a, b) in enumerate(copies)]
    for c in copies:
        c.start()
    for c in copies:
        c.wait()


def solution(mesh):
    nlon, nlat = mesh.shape["lon"], mesh.shape["lat"]
    f32, bf16 = jnp.float32, jnp.bfloat16
    rows = jax.ShapeDtypeStruct((ROWS, LEVELS, COLS), f32)
    block = jax.ShapeDtypeStruct((LEVELS, ROWS, COLS), f32)
    plane = jax.ShapeDtypeStruct((ROWS, COLS), f32)
    anywhere, vmem = pl.BlockSpec(memory_space=pl.ANY), pl.BlockSpec(memory_space=pltpu.VMEM)
    dma = pltpu.SemaphoreType.DMA

    def local(*args):
        args = [pltpu.with_memory_space_constraint(a, pltpu.HBM) for a in (*args[:-1], args[-1].T)]
        columns = pl.pallas_call(
            functools.partial(exchange, nlon, nlat),
            out_shape=(rows, rows, jax.ShapeDtypeStruct((3, ROWS, COLS), f32)),
            in_specs=[anywhere] * 10,
            out_specs=(vmem,) * 3,
            scratch_shapes=[
                pltpu.VMEM((4, ROWS + 2, LEVELS, COLS), f32),
                pltpu.VMEM((2, ROWS, LEVELS, COLS), f32),
                pltpu.VMEM((FIELDS, 3 * ROWS, COLS), f32),
                pltpu.VMEM((ROWS, COLS), jnp.int32),
                pltpu.VMEM((2 * LEVELS, HID), bf16),
                pltpu.VMEM((HID, 2 * LEVELS), bf16),
                pltpu.VMEM((LEVELS, HID), bf16),
                pltpu.VMEM((ROWS + 2, 8, COLS), f32),
                pltpu.VMEM((ROWS, 8, COLS), f32),
                pltpu.VMEM((2, 24, TILE), f32),
                pltpu.VMEM((2, 24, TILE), f32),
                pltpu.VMEM((4, 8, TILE), f32),
                dma((9,)),
                dma((6,)),
                dma((2,)),
                dma((8,)),
                dma((8,)),
                pltpu.SemaphoreType.REGULAR,
                pltpu.SemaphoreType.REGULAR,
            ],
            compiler_params=pltpu.CompilerParams(
                collective_id=0, has_side_effects=True, vmem_limit_bytes=LIMIT
            ),
        )(*args)
        return pl.pallas_call(
            deliver,
            out_shape=(block, block, plane, plane, plane),
            in_specs=[vmem] * 3,
            out_specs=(anywhere,) * 5,
            scratch_shapes=[dma((2 * ROWS + 3,))],
            compiler_params=pltpu.CompilerParams(vmem_limit_bytes=LIMIT),
        )(*columns)

    split, flat = P(None, "lat", "lon"), P("lat", "lon")
    return jax.shard_map(
        local,
        mesh=mesh,
        in_specs=(split,) * 4 + (flat,) * 4 + (P(), P()),
        out_specs=(split, split, flat, flat, flat),
        check_vma=False,
    )
```

```python
import functools

import jax
import jax.numpy as jnp
from jax import lax
from jax.experimental import pallas as pl
from jax.experimental.pallas import tpu as pltpu
from jax.sharding import PartitionSpec as P

MESH = pl.DeviceIdType.MESH
SUBSTEPS = 4
ADVECT = 0.1 * 0.25
SMOOTHING = 0.1
GRAVITY = 0.3 * 0.5
SPREADING = 0.3 * 0.5
BUOYANCY = 0.5 * 0.5
THERMAL = 0.2
HALINE = 0.15
MIXING_MAX = 0.45
LIMIT = 40 * 2**20
PERIOD = 16
LEVELS, ROWS, COLS, HID = 64, 8, 256, 256
GROUPS = LEVELS // 8
TILE = 128
U, T, S, V = range(4)
HEIGHT, EAST, NORTH, BUOYANT, DEPTH = range(5)
FIELDS = 5
E, W, N, S_, NE, SE, NW, SW = range(8)


def turn(x, shift, axis):
    size = x.shape[axis]
    return pltpu.roll(x, shift % size if isinstance(shift, int) else lax.rem(shift, size), axis)


def lanes_of(shape):
    return lax.broadcasted_iota(jnp.int32, shape, 1)


def levels_of(cols):
    return lax.broadcasted_iota(jnp.int32, (LEVELS, cols), 0).astype(jnp.float32)


def tall(block):
    return jnp.concatenate([block] * GROUPS, 0)


def network(w1_t, w2_t, thermal, saline):
    entries = jnp.concatenate([thermal, saline], 0).astype(jnp.bfloat16)
    hidden = jnp.tanh(jnp.dot(w1_t, entries, preferred_element_type=jnp.float32))
    return jnp.dot(
        w2_t, hidden.astype(jnp.bfloat16), preferred_element_type=jnp.float32
    )


def mixing(logits):
    return (0.5 * MIXING_MAX) * (1.0 + jnp.tanh(0.5 * logits))


def settle(tracer, kappa):
    flux = kappa * (turn(tracer, -1, 0) - tracer)
    return tracer + flux - turn(flux, 1, 0)


def face(lower, upper, speed, shared):
    return jnp.where(
        shared, ADVECT * speed * (lower + upper) - SMOOTHING * (upper - lower), 0.0
    )


def packed(vreg_of, slots, lane, rows):
    where = lanes_of((8, TILE))
    halves = []
    for r in range(2):
        total = None
        for g in range(4):
            part = None
            for a in range(slots):
                for j in rows:
                    target = 32 * g + 8 * a + j
                    moved = turn(vreg_of(a, j, 2 * g + r), target - lane + TILE, 1)
                    base = jnp.zeros_like(moved) if part is None else part
                    part = jnp.where(where == target, moved, base)
            total = part if total is None else total + part
        halves.append(total)
    return jnp.concatenate(halves, 0)


def unfolded(folded):
    return jnp.concatenate([turn(folded, -32 * g, 1) for g in range(4)], 0)


def edge_flux(lower, upper):
    first = lanes_of(lower.shape) % 32 < 8
    total, both = lower + upper, lower * upper
    speed = jnp.where(first, turn(total, -16, 1), turn(total, -8, 1))
    shared = jnp.where(first, turn(both, -24, 1), turn(both, -16, 1))
    return shared * (ADVECT * speed * total - SMOOTHING * (upper - lower))


def exchange(
    nlon, nlat,
    t, s, u, v, depth, height, east, north, w1, w2,
    out_t, out_s, out_surface,
    x, side, surface, depth_int, w1_in, w1_t, w2_t, deep, deep_east, lon_out, lon_in, corner_in,
    load_sem, row_send, row_recv, depth_send, depth_recv, send_sem, recv_sem, seam_sem, ready_sem,
):
    lon, lat = lax.axis_index("lon"), lax.axis_index("lat")
    z = lax.rem(lon, PERIOD)
    early, late, before = z == 0, z == PERIOD - 1, z == PERIOD - 2
    has_n, has_s = lat < nlat - 1, lat > 0
    sides = has_n.astype(jnp.int32) + has_s.astype(jnp.int32)
    to_east, to_west = lax.rem(lon + 1, nlon), lax.rem(lon + nlon - 1, nlon)
    device = {
        E: {"lon": to_east},
        W: {"lon": to_west},
        N: {"lat": lat + 1},
        S_: {"lat": lat - 1},
        NE: {"lon": to_east, "lat": lat + 1},
        SE: {"lon": to_east, "lat": lat - 1},
        NW: {"lon": to_west, "lat": lat + 1},
        SW: {"lon": to_west, "lat": lat - 1},
    }
    there = {E: True, W: True, N: has_n, NE: has_n, NW: has_n, S_: has_s, SE: has_s, SW: has_s}

    def signal(sem, way, also=True):
        @pl.when(jnp.logical_and(there[way], also))
        def _():
            pl.semaphore_signal(sem, inc=1, device_id=device[way], device_id_type=MESH)

    local = pltpu.make_async_copy
    plane = pl.ds(ROWS, ROWS)
    depth_load = local(depth, depth_int, load_sem.at[0])
    surface_loads = [
        local(f, surface.at[k, plane], load_sem.at[1 + k])
        for k, f in enumerate((height, east, north))
    ]

    def load_half(half, fields, sem):
        cut = pl.ds(half * TILE, TILE)
        for k, f in fields:
            for j in range(ROWS):
                local(f.at[:, j, cut], x.at[k, j + 1, :, cut], load_sem.at[sem]).start()

    def wait_half(half, k, count, sem):
        whole = x.at[pl.ds(k, count), pl.ds(1, ROWS), :, pl.ds(half * TILE, TILE)]
        local(whole, whole, load_sem.at[sem]).wait()

    depth_load.start()
    load_half(1, ((T, t), (S, s)), 4)
    for c in surface_loads:
        c.start()
    load_half(1, ((U, u),), 5)

    barrier = pltpu.get_barrier_semaphore()
    signal(barrier, W)
    signal(barrier, NW)
    signal(barrier, SW)
    usual = jnp.logical_not(late)
    both = jnp.logical_and
    place, half_one = lax.rem(lat, 4), lon < nlon // 2
    north_first = jnp.where(place == 3, half_one, place != 1)
    south_first = jnp.where(place == 0, jnp.logical_not(half_one), place == 2)
    last_in_pair_n, last_in_pair_s = north_first, south_first
    signal(barrier, E, usual)
    signal(barrier, N, jnp.logical_or(usual, jnp.logical_not(last_in_pair_n)))
    signal(barrier, S_, jnp.logical_or(usual, jnp.logical_not(last_in_pair_s)))
    signal(barrier, NE, both(usual, jnp.logical_not(both(before, last_in_pair_n))))
    signal(barrier, SE, both(usual, jnp.logical_not(both(before, last_in_pair_s))))

    load_half(0, ((T, t), (S, s), (U, u)), 6)
    for j in range(ROWS):
        local(v.at[:, j, :], x.at[V, j + 1], load_sem.at[7]).start()
    weights = [local(w1, w1_in, load_sem.at[8]), local(w2, w2_t, load_sem.at[9])]
    for c in weights:
        c.start()

    count_n, count_s = has_n.astype(jnp.int32), has_s.astype(jnp.int32)
    firsts = jnp.where(north_first, count_n, 0) + jnp.where(south_first, count_s, 0)
    expected = jnp.where(early, 1 + 2 * sides, jnp.where(late, 2 + sides + 2 * firsts, 2 + 3 * sides))

    @pl.when(usual)
    def _():
        pl.semaphore_wait(barrier, expected)

    signal(ready_sem, NE, both(before, last_in_pair_n))
    signal(ready_sem, SE, both(before, last_in_pair_s))

    remote = pltpu.make_async_remote_copy

    def row_copies(way):
        source, target = (ROWS - 1, 0) if way == N else (0, ROWS + 1)
        k = way - N
        return [
            remote(f.at[:, source, :], x.at[a, target], row_send.at[3 * k + i], row_recv.at[1 - k],
                   device_id=device[way], device_id_type=MESH)
            for i, (a, f) in enumerate(((T, t), (S, s), (V, v)))
        ]

    opposite = {E: W, W: E, N: S_, S_: N, NE: SW, SW: NE, NW: SE, SE: NW}
    lon_slot = {E: 0, W: 1}
    corner_slot = {NE: 0, SE: 1, NW: 2, SW: 3}
    surface_rows = {N: pl.ds(2 * ROWS, ROWS), S_: pl.ds(0, ROWS)}
    tail = pl.ds(16, 8)

    def message(way):
        if way in lon_slot:
            src, dst = lon_out.at[lon_slot[way]], lon_in.at[lon_slot[opposite[way]]]
        elif way in corner_slot:
            src = lon_out.at[0 if way in (NE, SE) else 1, tail]
            dst = corner_in.at[corner_slot[opposite[way]]]
        else:
            most = pl.ds(0, FIELDS - 1)
            src, dst = surface.at[most, plane], surface.at[most, surface_rows[opposite[way]]]
        return remote(src, dst, send_sem.at[way], recv_sem.at[opposite[way]],
                      device_id=device[way], device_id_type=MESH)

    def depth_message(way):
        k = way - N
        return remote(surface.at[DEPTH, plane], surface.at[DEPTH, surface_rows[opposite[way]]],
                      depth_send.at[k], depth_recv.at[1 - k], device_id=device[way], device_id_type=MESH)

    def send_depth(also):
        for way in (N, S_):

            @pl.when(jnp.logical_and(there[way], also))
            def _(way=way):
                depth_message(way).start()

    def send(way, also=True):
        @pl.when(jnp.logical_and(there[way], also))
        def _():
            message(way).start()

    def send_rows(also):
        for way in (N, S_):

            @pl.when(jnp.logical_and(there[way], also))
            def _(way=way):
                for c in row_copies(way):
                    c.start()

    send_rows(usual)

    @pl.when(jnp.logical_not(has_s))
    def _():
        x[:, 0] = jnp.zeros((4, LEVELS, COLS), jnp.float32)
        surface[:, 0:ROWS] = jnp.zeros((FIELDS, ROWS, COLS), jnp.float32)
        corner_in[1] = jnp.zeros((8, TILE), jnp.float32)
        corner_in[3] = jnp.zeros((8, TILE), jnp.float32)

    @pl.when(jnp.logical_not(has_n))
    def _():
        x[:, ROWS + 1] = jnp.zeros((4, LEVELS, COLS), jnp.float32)
        surface[:, 2 * ROWS : 3 * ROWS] = jnp.zeros((FIELDS, ROWS, COLS), jnp.float32)
        corner_in[0] = jnp.zeros((8, TILE), jnp.float32)
        corner_in[2] = jnp.zeros((8, TILE), jnp.float32)

    depth_load.wait()
    deeps = depth_int[...].astype(jnp.float32)
    surface[DEPTH, plane] = deeps
    beside = jnp.where(lanes_of((ROWS, COLS)) == COLS - 1, 0.0, turn(deeps, -1, 1))
    beside = jnp.minimum(deeps, beside)
    for j in range(ROWS):
        deep[j + 1] = jnp.broadcast_to(deeps[j : j + 1], (8, COLS))
        deep_east[j] = jnp.broadcast_to(beside[j : j + 1], (8, COLS))

    def pack_half(half):
        cut = pl.ds(half * TILE, TILE)
        edge = TILE - 1 if half else 0
        level = lax.broadcasted_iota(jnp.int32, (8, TILE), 0).astype(jnp.float32)
        where = lanes_of((8, TILE))

        def wet(j, q):
            return level + 8.0 * q < deep[j + 1, :, cut]

        def vreg(a, j, q):
            if a == 3:
                return jnp.where(wet(j, q), 1.0, 0.0)
            return x[(T, S, U)[a], j + 1, pl.ds(8 * q, 8), cut]

        def surface_part():
            for j in range(ROWS):
                total = jnp.zeros((8, TILE), jnp.float32)
                for q in range(GROUPS):
                    rows = pl.ds(8 * q, 8)
                    density = THERMAL * x[T, j + 1, rows, cut] - HALINE * x[S, j + 1, rows, cut]
                    total = total + jnp.where(wet(j, q), density, 0.0)
                surface[BUOYANT, ROWS + j : ROWS + j + 1, cut] = (LEVELS**-0.5) * jnp.sum(total, 0, keepdims=True)
            kept = (where >= TILE - 8) if half else (where < 8)
            lon_out[1 - half, 16:24] = sum(
                turn(jnp.where(kept, surface[f, plane, cut], 0.0), 16 * f, 1)
                for f in range(FIELDS)
            )

        def tracer_part():
            lon_out[1 - half, 0:16] = packed(vreg, 4, edge, range(ROWS))

        return surface_part, tracer_part

    surface_part, tracer_part = pack_half(1)
    wait_half(1, T, 2, 4)
    for c in surface_loads:
        c.wait()
    surface_part()

    @pl.when(late)
    def _():
        pl.semaphore_wait(barrier, expected)

    send(NE)
    send(SE)
    wait_half(1, U, 1, 5)
    tracer_part()
    send(E)
    for way in (E, NE, SE):
        signal(seam_sem, way, late)
    signal(ready_sem, N, both(late, last_in_pair_n))
    signal(ready_sem, S_, both(late, last_in_pair_s))
    send_depth(usual)
    wait_half(0, U, 3, 6)
    for part in pack_half(0):
        part()
    send(W, jnp.logical_not(early))
    middle = jnp.logical_and(usual, jnp.logical_not(early))
    send(NW, middle)
    send(SW, middle)

    lasts = jnp.where(north_first, 0, count_n) + jnp.where(south_first, 0, count_s)

    @pl.when(both(late, lasts > 0))
    def _():
        pl.semaphore_wait(ready_sem, 2 * lasts)

    send_rows(late)
    send_depth(late)
    send(NW, late)
    send(SW, late)

    for c in weights:
        c.wait()
    w1_t[...] = w1_in[...].astype(jnp.float32).T.astype(jnp.bfloat16)
    all_v = x.at[V, pl.ds(1, ROWS)]
    local(all_v, all_v, load_sem.at[7]).wait()

    def row(j):
        level = levels_of(COLS)
        speed = x[U, j + 1]
        speed = speed + turn(speed, -1, 1)
        here, above, below = deep[j + 1], deep[j + 2], deep[j]
        open_east = level < tall(deep_east[j])
        open_north = level < tall(jnp.minimum(here, above))
        open_south = level < tall(jnp.minimum(here, below))
        wet = level < tall(here)
        wet_below = level + 1.0 < tall(here)
        speed_north = x[V, j + 1] + x[V, j + 2]
        speed_south = x[V, j + 1] + x[V, j]

        def lateral(k):
            own = x[k, j + 1]
            flux = face(own, turn(own, -1, 1), speed, open_east)
            return own - (
                flux
                - turn(flux, 1, 1)
                + face(own, x[k, j + 2], speed_north, open_north)
                - face(x[k, j], own, speed_south, open_south)
            )

        thermal, saline = lateral(T), lateral(S)
        side[0, j] = thermal
        side[1, j] = saline
        logits = network(
            w1_t[...], w2_t[...], jnp.where(wet, thermal, 0.0), jnp.where(wet, saline, 0.0)
        )
        kappa = jnp.where(wet_below, mixing(logits), 0.0)
        out_t[j] = settle(thermal, kappa)
        out_s[j] = settle(saline, kappa)

    pl.loop(1, ROWS - 1)(row)
    send(N)
    send(S_)

    def side_pack(half, rows):
        cut = pl.ds(half * TILE, TILE)
        return packed(
            lambda a, j, q: side[a, j, pl.ds(8 * q, 8), cut],
            2,
            TILE - 1 if half else 0,
            rows,
        )

    inside = range(1, ROWS - 1)
    part_east, part_west = side_pack(1, inside), side_pack(0, inside)

    near_north = lax.rem(lat, 2) == 0

    def outer(north):
        for way in (N, S_):

            @pl.when(jnp.logical_and(there[way], north if way == N else jnp.logical_not(north)))
            def _(way=way):
                k = way - N
                rows = x.at[pl.ds(T, 3), ROWS + 1 if way == N else 0]
                local(rows, rows, row_recv.at[k]).wait()
                depth_message(opposite[way]).wait_recv()

        edge = jnp.where(north, ROWS - 1, 0)
        beyond = jnp.where(north, 2 * ROWS, ROWS - 1)
        deep[jnp.where(north, ROWS + 1, 0)] = jnp.broadcast_to(surface[DEPTH, pl.ds(beyond, 1)], (8, COLS))
        row(edge)
        return side_pack(1, [edge]), side_pack(0, [edge])

    near_east, near_west = outer(near_north)
    far_east, far_west = outer(jnp.logical_not(near_north))
    part_east = part_east + near_east + far_east
    part_west = part_west + near_west + far_west

    @pl.when(early)
    def _():
        pl.semaphore_wait(seam_sem, 1 + sides)

    for way in (W, NW, SW):
        send(way, early)

    for way in (E, W):
        message(opposite[way]).wait_recv()

    own_east, own_west = lon_out[0, 0:16], lon_out[1, 0:16]
    from_east, from_west = lon_in[0, 0:16], lon_in[1, 0:16]
    at_east = part_east - edge_flux(own_east, from_east)
    at_west = part_west + edge_flux(from_west, own_west)
    lane16 = lanes_of((16, TILE))
    first_slot = lane16 % 32 < 8
    thermal = unfolded(jnp.where(first_slot, at_west, turn(at_east, 8, 1)))
    saline = unfolded(jnp.where(first_slot, turn(at_west, -8, 1), at_east))
    wet = unfolded(jnp.where(first_slot, turn(own_west, -24, 1), turn(own_east, -16, 1)))
    lane = lanes_of((LEVELS, TILE))
    wet = jnp.where(lane < 16, wet, 0.0)
    wet_below = jnp.where(levels_of(TILE) < LEVELS - 1.0, turn(wet, -1, 0), 0.0)
    logits = network(w1_t[...], w2_t[...], thermal * wet, saline * wet)
    kappa = mixing(logits) * wet * wet_below
    for out, tracer in ((out_t, thermal), (out_s, saline)):
        new = settle(tracer, kappa)
        for j in range(ROWS):
            out[j, :, 0:TILE] = jnp.where(lane == 0, turn(new, -j, 1), out[j, :, 0:TILE])
            out[j, :, TILE:] = jnp.where(lane == TILE - 1, turn(new, TILE - 1 - 8 - j, 1), out[j, :, TILE:])

    for way in (N, S_, NE, SE, NW, SW):

        @pl.when(there[way])
        def _(way=way):
            message(opposite[way]).wait_recv()

    third = jnp.concatenate(
        [
            corner_in[1] + corner_in[3],
            lon_in[0, 16:24] + lon_in[1, 16:24],
            corner_in[0] + corner_in[2],
        ],
        0,
    )
    where = lanes_of((3 * ROWS, TILE))
    around = jnp.logical_or(where < 8, where >= TILE - 8)
    field = [
        jnp.concatenate([surface[f], jnp.where(around, turn(third, -16 * f, 1), 0.0)], 1)
        for f in range(FIELDS)
    ]
    h, e, n, b, d = field
    land = d <= 0.0
    column = d * (1.0 / LEVELS)

    def eastward(a):
        return turn(a, -1, 1) - turn(a, 1, 1)

    def northward(a):
        return turn(a, -1, 0) - turn(a, 1, 0)

    east_force, north_force = -BUOYANCY * eastward(b), -BUOYANCY * northward(b)
    for _ in range(SUBSTEPS):
        e = jnp.where(land, 0.0, e - GRAVITY * eastward(h) + east_force)
        n = jnp.where(land, 0.0, n - GRAVITY * northward(h) + north_force)
        h = jnp.where(land, 0.0, h - SPREADING * (eastward(column * e) + northward(column * n)))
    for k, a in enumerate((h, e, n)):
        out_surface[k] = a[ROWS : 2 * ROWS, 0:COLS]

    for way in (N, S_):

        @pl.when(there[way])
        def _(way=way):
            for c in row_copies(way):
                c.wait_send()
            depth_message(way).wait_send()

    for way in range(8):

        @pl.when(there[way])
        def _(way=way):
            message(way).wait_send()


def deliver(t, s, surface, out_t, out_s, height, east, north, sem):
    copies = []
    for src, dst in ((t, out_t), (s, out_s)):
        copies += [(src.at[j], dst.at[:, j, :]) for j in range(ROWS)]
    copies += [(surface.at[k], dst) for k, dst in enumerate((height, east, north))]
    copies = [pltpu.make_async_copy(a, b, sem.at[i]) for i, (a, b) in enumerate(copies)]
    for c in copies:
        c.start()
    for c in copies:
        c.wait()


def solution(mesh):
    nlon, nlat = mesh.shape["lon"], mesh.shape["lat"]
    f32, bf16 = jnp.float32, jnp.bfloat16
    rows = jax.ShapeDtypeStruct((ROWS, LEVELS, COLS), f32)
    block = jax.ShapeDtypeStruct((LEVELS, ROWS, COLS), f32)
    plane = jax.ShapeDtypeStruct((ROWS, COLS), f32)
    anywhere, vmem = pl.BlockSpec(memory_space=pl.ANY), pl.BlockSpec(memory_space=pltpu.VMEM)
    dma = pltpu.SemaphoreType.DMA

    def local(*args):
        args = [pltpu.with_memory_space_constraint(a, pltpu.HBM) for a in (*args[:-1], args[-1].T)]
        columns = pl.pallas_call(
            functools.partial(exchange, nlon, nlat),
            out_shape=(rows, rows, jax.ShapeDtypeStruct((3, ROWS, COLS), f32)),
            in_specs=[anywhere] * 10,
            out_specs=(vmem,) * 3,
            scratch_shapes=[
                pltpu.VMEM((4, ROWS + 2, LEVELS, COLS), f32),
                pltpu.VMEM((2, ROWS, LEVELS, COLS), f32),
                pltpu.VMEM((FIELDS, 3 * ROWS, COLS), f32),
                pltpu.VMEM((ROWS, COLS), jnp.int32),
                pltpu.VMEM((2 * LEVELS, HID), bf16),
                pltpu.VMEM((HID, 2 * LEVELS), bf16),
                pltpu.VMEM((LEVELS, HID), bf16),
                pltpu.VMEM((ROWS + 2, 8, COLS), f32),
                pltpu.VMEM((ROWS, 8, COLS), f32),
                pltpu.VMEM((2, 24, TILE), f32),
                pltpu.VMEM((2, 24, TILE), f32),
                pltpu.VMEM((4, 8, TILE), f32),
                dma((10,)),
                dma((6,)),
                dma((2,)),
                dma((2,)),
                dma((2,)),
                dma((8,)),
                dma((8,)),
                pltpu.SemaphoreType.REGULAR,
                pltpu.SemaphoreType.REGULAR,
            ],
            compiler_params=pltpu.CompilerParams(
                collective_id=0, has_side_effects=True, vmem_limit_bytes=LIMIT
            ),
        )(*args)
        return pl.pallas_call(
            deliver,
            out_shape=(block, block, plane, plane, plane),
            in_specs=[vmem] * 3,
            out_specs=(anywhere,) * 5,
            scratch_shapes=[dma((2 * ROWS + 3,))],
            compiler_params=pltpu.CompilerParams(vmem_limit_bytes=LIMIT),
        )(*columns)

    split, flat = P(None, "lat", "lon"), P("lat", "lon")
    return jax.shard_map(
        local,
        mesh=mesh,
        in_specs=(split,) * 4 + (flat,) * 4 + (P(), P()),
        out_specs=(split, split, flat, flat, flat),
        check_vma=False,
    )
```

```python
import functools

import jax
import jax.numpy as jnp
from jax import lax
from jax.experimental import pallas as pl
from jax.experimental.pallas import tpu as pltpu
from jax.sharding import PartitionSpec as P

MESH = pl.DeviceIdType.MESH
SUBSTEPS = 4
ADVECT = 0.1 * 0.25
SMOOTHING = 0.1
GRAVITY = 0.3 * 0.5
SPREADING = 0.3 * 0.5
BUOYANCY = 0.5 * 0.5
THERMAL = 0.2
HALINE = 0.15
MIXING_MAX = 0.45
LIMIT = 40 * 2**20
PERIOD = 16
LEVELS, ROWS, COLS, HID = 64, 8, 256, 256
GROUPS = LEVELS // 8
TILE = 128
U, T, S, V = range(4)
HEIGHT, EAST, NORTH, BUOYANT, DEPTH = range(5)
FIELDS = 5
E, W, N, S_, NE, SE, NW, SW = range(8)


def turn(x, shift, axis):
    size = x.shape[axis]
    return pltpu.roll(x, shift % size if isinstance(shift, int) else lax.rem(shift, size), axis)


def lanes_of(shape):
    return lax.broadcasted_iota(jnp.int32, shape, 1)


def levels_of(cols):
    return lax.broadcasted_iota(jnp.int32, (LEVELS, cols), 0).astype(jnp.float32)


def tall(block):
    return jnp.concatenate([block] * GROUPS, 0)


def network(w1_t, w2_t, thermal, saline):
    entries = jnp.concatenate([thermal, saline], 0).astype(jnp.bfloat16)
    hidden = jnp.tanh(jnp.dot(w1_t, entries, preferred_element_type=jnp.float32))
    return jnp.dot(
        w2_t, hidden.astype(jnp.bfloat16), preferred_element_type=jnp.float32
    )


def mixing(logits):
    return (0.5 * MIXING_MAX) * (1.0 + jnp.tanh(0.5 * logits))


def settle(tracer, kappa):
    flux = kappa * (turn(tracer, -1, 0) - tracer)
    return tracer + flux - turn(flux, 1, 0)


def face(lower, upper, speed, shared):
    return jnp.where(
        shared, ADVECT * speed * (lower + upper) - SMOOTHING * (upper - lower), 0.0
    )


def packed(vreg_of, slots, lane, rows):
    where = lanes_of((8, TILE))
    halves = []
    for r in range(2):
        total = None
        for g in range(4):
            part = None
            for a in range(slots):
                for j in rows:
                    target = 32 * g + 8 * a + j
                    moved = turn(vreg_of(a, j, 2 * g + r), target - lane + TILE, 1)
                    base = jnp.zeros_like(moved) if part is None else part
                    part = jnp.where(where == target, moved, base)
            total = part if total is None else total + part
        halves.append(total)
    return jnp.concatenate(halves, 0)


def unfolded(folded):
    return jnp.concatenate([turn(folded, -32 * g, 1) for g in range(4)], 0)


def edge_flux(lower, upper):
    first = lanes_of(lower.shape) % 32 < 8
    total, both = lower + upper, lower * upper
    speed = jnp.where(first, turn(total, -16, 1), turn(total, -8, 1))
    shared = jnp.where(first, turn(both, -24, 1), turn(both, -16, 1))
    return shared * (ADVECT * speed * total - SMOOTHING * (upper - lower))


def exchange(
    nlon, nlat,
    t, s, u, v, depth, height, east, north, w1, w2,
    out_t, out_s, out_surface,
    x, side, surface, depth_int, w1_in, w1_t, w2_t, deep, deep_east, lon_out, lon_in, corner_in,
    load_sem, row_send, row_recv, depth_send, depth_recv, send_sem, recv_sem, seam_sem, ready_sem, east_sem,
):
    lon, lat = lax.axis_index("lon"), lax.axis_index("lat")
    z = lax.rem(lon, PERIOD)
    early, late, before = z == 0, z == PERIOD - 1, z == PERIOD - 2
    has_n, has_s = lat < nlat - 1, lat > 0
    sides = has_n.astype(jnp.int32) + has_s.astype(jnp.int32)
    to_east, to_west = lax.rem(lon + 1, nlon), lax.rem(lon + nlon - 1, nlon)
    device = {
        E: {"lon": to_east},
        W: {"lon": to_west},
        N: {"lat": lat + 1},
        S_: {"lat": lat - 1},
        NE: {"lon": to_east, "lat": lat + 1},
        SE: {"lon": to_east, "lat": lat - 1},
        NW: {"lon": to_west, "lat": lat + 1},
        SW: {"lon": to_west, "lat": lat - 1},
    }
    there = {E: True, W: True, N: has_n, NE: has_n, NW: has_n, S_: has_s, SE: has_s, SW: has_s}

    def signal(sem, way, also=True):
        @pl.when(jnp.logical_and(there[way], also))
        def _():
            pl.semaphore_signal(sem, inc=1, device_id=device[way], device_id_type=MESH)

    local = pltpu.make_async_copy
    plane = pl.ds(ROWS, ROWS)
    depth_load = local(depth, depth_int, load_sem.at[0])
    surface_loads = [
        local(f, surface.at[k, plane], load_sem.at[1 + k])
        for k, f in enumerate((height, east, north))
    ]

    def load_half(half, fields, sem):
        cut = pl.ds(half * TILE, TILE)
        for k, f in fields:
            for j in range(ROWS):
                local(f.at[:, j, cut], x.at[k, j + 1, :, cut], load_sem.at[sem]).start()

    def wait_half(half, k, count, sem):
        whole = x.at[pl.ds(k, count), pl.ds(1, ROWS), :, pl.ds(half * TILE, TILE)]
        local(whole, whole, load_sem.at[sem]).wait()

    for c in (depth_load, *surface_loads):
        c.start()
    load_half(1, ((T, t), (S, s)), 4)
    load_half(1, ((U, u),), 5)

    barrier = pltpu.get_barrier_semaphore()
    usual = jnp.logical_not(late)
    both = jnp.logical_and
    inner = both(usual, jnp.logical_not(before))
    for way in (E, NE, SE):
        signal(barrier, way, inner)
    for way in (W, NW, SW):
        signal(barrier, way, jnp.logical_or(early, late))
    signal(barrier, N, usual)
    signal(barrier, S_, usual)
    expected = jnp.where(early, sides, jnp.where(late, 1 + sides, jnp.where(before, 2 + 3 * sides, 1 + 2 * sides)))
    pl.semaphore_wait(barrier, expected)
    signal(ready_sem, E, before)
    for way in (E, NE, SE):
        signal(seam_sem, way, late)
    for way in (W, NW, SW):
        signal(east_sem, way, jnp.logical_not(jnp.logical_or(early, late)))

    remote = pltpu.make_async_remote_copy

    def row_copies(way):
        source, target = (ROWS - 1, 0) if way == N else (0, ROWS + 1)
        k = way - N
        return [
            remote(f.at[:, source, :], x.at[a, target], row_send.at[3 * k + i], row_recv.at[1 - k],
                   device_id=device[way], device_id_type=MESH)
            for i, (a, f) in enumerate(((T, t), (S, s), (V, v)))
        ]

    opposite = {E: W, W: E, N: S_, S_: N, NE: SW, SW: NE, NW: SE, SE: NW}
    lon_slot = {E: 0, W: 1}
    corner_slot = {NE: 0, SE: 1, NW: 2, SW: 3}
    surface_rows = {N: pl.ds(2 * ROWS, ROWS), S_: pl.ds(0, ROWS)}
    tail = pl.ds(16, 8)

    def message(way):
        if way in lon_slot:
            src, dst = lon_out.at[lon_slot[way]], lon_in.at[lon_slot[opposite[way]]]
        elif way in corner_slot:
            src = lon_out.at[0 if way in (NE, SE) else 1, tail]
            dst = corner_in.at[corner_slot[opposite[way]]]
        else:
            most = pl.ds(0, FIELDS - 1)
            src, dst = surface.at[most, plane], surface.at[most, surface_rows[opposite[way]]]
        return remote(src, dst, send_sem.at[way], recv_sem.at[opposite[way]],
                      device_id=device[way], device_id_type=MESH)

    def depth_message(way):
        k = way - N
        return remote(surface.at[DEPTH, plane], surface.at[DEPTH, surface_rows[opposite[way]]],
                      depth_send.at[k], depth_recv.at[1 - k], device_id=device[way], device_id_type=MESH)

    def send_depth(also):
        for way in (N, S_):

            @pl.when(jnp.logical_and(there[way], also))
            def _(way=way):
                depth_message(way).start()

    def send(way, also=True):
        @pl.when(jnp.logical_and(there[way], also))
        def _():
            message(way).start()

    def send_rows(also):
        for way in (N, S_):

            @pl.when(jnp.logical_and(there[way], also))
            def _(way=way):
                for c in row_copies(way):
                    c.start()

    send_rows(usual)

    @pl.when(jnp.logical_not(has_s))
    def _():
        x[:, 0] = jnp.zeros((4, LEVELS, COLS), jnp.float32)
        surface[:, 0:ROWS] = jnp.zeros((FIELDS, ROWS, COLS), jnp.float32)
        corner_in[1] = jnp.zeros((8, TILE), jnp.float32)
        corner_in[3] = jnp.zeros((8, TILE), jnp.float32)

    @pl.when(jnp.logical_not(has_n))
    def _():
        x[:, ROWS + 1] = jnp.zeros((4, LEVELS, COLS), jnp.float32)
        surface[:, 2 * ROWS : 3 * ROWS] = jnp.zeros((FIELDS, ROWS, COLS), jnp.float32)
        corner_in[0] = jnp.zeros((8, TILE), jnp.float32)
        corner_in[2] = jnp.zeros((8, TILE), jnp.float32)

    depth_load.wait()
    deeps = depth_int[...].astype(jnp.float32)
    surface[DEPTH, plane] = deeps
    beside = jnp.where(lanes_of((ROWS, COLS)) == COLS - 1, 0.0, turn(deeps, -1, 1))
    beside = jnp.minimum(deeps, beside)
    for j in range(ROWS):
        deep[j + 1] = jnp.broadcast_to(deeps[j : j + 1], (8, COLS))
        deep_east[j] = jnp.broadcast_to(beside[j : j + 1], (8, COLS))

    def pack_half(half):
        cut = pl.ds(half * TILE, TILE)
        edge = TILE - 1 if half else 0
        level = lax.broadcasted_iota(jnp.int32, (8, TILE), 0).astype(jnp.float32)
        where = lanes_of((8, TILE))

        def wet(j, q):
            return level + 8.0 * q < deep[j + 1, :, cut]

        def vreg(a, j, q):
            if a == 3:
                return jnp.where(wet(j, q), 1.0, 0.0)
            return x[(T, S, U)[a], j + 1, pl.ds(8 * q, 8), cut]

        def surface_part():
            for j in range(ROWS):
                total = jnp.zeros((8, TILE), jnp.float32)
                for q in range(GROUPS):
                    rows = pl.ds(8 * q, 8)
                    density = THERMAL * x[T, j + 1, rows, cut] - HALINE * x[S, j + 1, rows, cut]
                    total = total + jnp.where(wet(j, q), density, 0.0)
                surface[BUOYANT, ROWS + j : ROWS + j + 1, cut] = (LEVELS**-0.5) * jnp.sum(total, 0, keepdims=True)
            kept = (where >= TILE - 8) if half else (where < 8)
            lon_out[1 - half, 16:24] = sum(
                turn(jnp.where(kept, surface[f, plane, cut], 0.0), 16 * f, 1)
                for f in range(FIELDS)
            )

        def tracer_part():
            lon_out[1 - half, 0:16] = packed(vreg, 4, edge, range(ROWS))

        return surface_part, tracer_part

    surface_part, tracer_part = pack_half(1)
    wait_half(1, T, 2, 4)
    for c in surface_loads:
        c.wait()
    surface_part()
    at_once = jnp.logical_not(inner)
    send(NE, at_once)
    send(SE, at_once)
    wait_half(1, U, 1, 5)
    tracer_part()
    send(E, at_once)
    load_half(0, ((T, t), (S, s), (U, u)), 6)
    for j in range(ROWS):
        local(v.at[:, j, :], x.at[V, j + 1], load_sem.at[7]).start()
    weights = [local(w1, w1_in, load_sem.at[8]), local(w2, w2_t, load_sem.at[9])]
    for c in weights:
        c.start()
    send_depth(usual)
    wait_half(0, U, 3, 6)
    for part in pack_half(0):
        part()
    middle = jnp.logical_and(usual, jnp.logical_not(early))
    for way in (W, NW, SW):
        send(way, middle)

    @pl.when(late)
    def _():
        pl.semaphore_wait(ready_sem, 1)

    send_rows(late)
    send_depth(late)
    for way in (W, NW, SW):
        send(way, late)

    for c in weights:
        c.wait()
    w1_t[...] = w1_in[...].astype(jnp.float32).T.astype(jnp.bfloat16)
    all_v = x.at[V, pl.ds(1, ROWS)]
    local(all_v, all_v, load_sem.at[7]).wait()

    def row(j):
        level = levels_of(COLS)
        speed = x[U, j + 1]
        speed = speed + turn(speed, -1, 1)
        here, above, below = deep[j + 1], deep[j + 2], deep[j]
        open_east = level < tall(deep_east[j])
        open_north = level < tall(jnp.minimum(here, above))
        open_south = level < tall(jnp.minimum(here, below))
        wet = level < tall(here)
        wet_below = level + 1.0 < tall(here)
        speed_north = x[V, j + 1] + x[V, j + 2]
        speed_south = x[V, j + 1] + x[V, j]

        def lateral(k):
            own = x[k, j + 1]
            flux = face(own, turn(own, -1, 1), speed, open_east)
            return own - (
                flux
                - turn(flux, 1, 1)
                + face(own, x[k, j + 2], speed_north, open_north)
                - face(x[k, j], own, speed_south, open_south)
            )

        thermal, saline = lateral(T), lateral(S)
        side[0, j] = thermal
        side[1, j] = saline
        logits = network(
            w1_t[...], w2_t[...], jnp.where(wet, thermal, 0.0), jnp.where(wet, saline, 0.0)
        )
        kappa = jnp.where(wet_below, mixing(logits), 0.0)
        out_t[j] = settle(thermal, kappa)
        out_s[j] = settle(saline, kappa)

    pl.loop(1, ROWS - 1)(row)

    @pl.when(inner)
    def _():
        pl.semaphore_wait(east_sem, 1 + sides)

    for way in (E, NE, SE):
        send(way, inner)
    send(N)
    send(S_)

    def side_pack(half, rows):
        cut = pl.ds(half * TILE, TILE)
        return packed(
            lambda a, j, q: side[a, j, pl.ds(8 * q, 8), cut],
            2,
            TILE - 1 if half else 0,
            rows,
        )

    inside = range(1, ROWS - 1)
    part_east, part_west = side_pack(1, inside), side_pack(0, inside)

    near_north = lax.rem(lat, 2) == 0

    def outer(north):
        for way in (N, S_):

            @pl.when(jnp.logical_and(there[way], north if way == N else jnp.logical_not(north)))
            def _(way=way):
                k = way - N
                rows = x.at[pl.ds(T, 3), ROWS + 1 if way == N else 0]
                local(rows, rows, row_recv.at[k]).wait()
                depth_message(opposite[way]).wait_recv()

        edge = jnp.where(north, ROWS - 1, 0)
        beyond = jnp.where(north, 2 * ROWS, ROWS - 1)
        deep[jnp.where(north, ROWS + 1, 0)] = jnp.broadcast_to(surface[DEPTH, pl.ds(beyond, 1)], (8, COLS))
        row(edge)
        return side_pack(1, [edge]), side_pack(0, [edge])

    near_east, near_west = outer(near_north)
    far_east, far_west = outer(jnp.logical_not(near_north))
    part_east = part_east + near_east + far_east
    part_west = part_west + near_west + far_west

    @pl.when(early)
    def _():
        pl.semaphore_wait(seam_sem, 1 + sides)

    for way in (W, NW, SW):
        send(way, early)

    for way in (E, W):
        message(opposite[way]).wait_recv()

    own_east, own_west = lon_out[0, 0:16], lon_out[1, 0:16]
    from_east, from_west = lon_in[0, 0:16], lon_in[1, 0:16]
    at_east = part_east - edge_flux(own_east, from_east)
    at_west = part_west + edge_flux(from_west, own_west)
    lane16 = lanes_of((16, TILE))
    first_slot = lane16 % 32 < 8
    thermal = unfolded(jnp.where(first_slot, at_west, turn(at_east, 8, 1)))
    saline = unfolded(jnp.where(first_slot, turn(at_west, -8, 1), at_east))
    wet = unfolded(jnp.where(first_slot, turn(own_west, -24, 1), turn(own_east, -16, 1)))
    lane = lanes_of((LEVELS, TILE))
    wet = jnp.where(lane < 16, wet, 0.0)
    wet_below = jnp.where(levels_of(TILE) < LEVELS - 1.0, turn(wet, -1, 0), 0.0)
    logits = network(w1_t[...], w2_t[...], thermal * wet, saline * wet)
    kappa = mixing(logits) * wet * wet_below
    for out, tracer in ((out_t, thermal), (out_s, saline)):
        new = settle(tracer, kappa)
        for j in range(ROWS):
            out[j, :, 0:TILE] = jnp.where(lane == 0, turn(new, -j, 1), out[j, :, 0:TILE])
            out[j, :, TILE:] = jnp.where(lane == TILE - 1, turn(new, TILE - 1 - 8 - j, 1), out[j, :, TILE:])

    for way in (N, S_, NE, SE, NW, SW):

        @pl.when(there[way])
        def _(way=way):
            message(opposite[way]).wait_recv()

    third = jnp.concatenate(
        [
            corner_in[1] + corner_in[3],
            lon_in[0, 16:24] + lon_in[1, 16:24],
            corner_in[0] + corner_in[2],
        ],
        0,
    )
    where = lanes_of((3 * ROWS, TILE))
    around = jnp.logical_or(where < 8, where >= TILE - 8)
    field = [
        jnp.concatenate([surface[f], jnp.where(around, turn(third, -16 * f, 1), 0.0)], 1)
        for f in range(FIELDS)
    ]
    h, e, n, b, d = field
    def ahead_behind(a, axis, by):
        return turn(a, -by, axis), turn(a, by, axis)

    def current(flow, axis):
        flows, depths = ahead_behind(flow, axis, 1), ahead_behind(d, axis, 1)
        after, before_ = ahead_behind(b, axis, 2)
        forces = -BUOYANCY * (after - b), -BUOYANCY * (b - before_)
        return [
            (f, g, p <= 0.0, p * (1.0 / LEVELS)) for f, g, p in zip(flows, forces, depths)
        ]

    land = d <= 0.0
    state = {1: current(e, 1), 0: current(n, 0)}
    for step in range(SUBSTEPS):
        carried = 0.0
        if step == SUBSTEPS - 1:
            (e, force, _, _), (n, force_n, _, _) = state[1][0], state[0][0]
            e, n = turn(e, 1, 1), turn(n, 1, 0)
            rises = [ahead_behind(h, axis, 1) for axis in (1, 0)]
            e = e - GRAVITY * (rises[0][0] - rises[0][1]) + turn(force, 1, 1)
            n = n - GRAVITY * (rises[1][0] - rises[1][1]) + turn(force_n, 1, 0)
            e, n = jnp.where(land, 0.0, e), jnp.where(land, 0.0, n)
        for axis in (1, 0):
            after, before_ = ahead_behind(h, axis, 2)
            slopes = after - h, h - before_
            state[axis] = [
                (jnp.where(dry, 0.0, f - GRAVITY * slope + g), g, dry, c)
                for (f, g, dry, c), slope in zip(state[axis], slopes)
            ]
            (ahead, _, _, c_ahead), (behind, _, _, c_behind) = state[axis]
            carried = carried + (c_ahead * ahead - c_behind * behind)
        h = jnp.where(land, 0.0, h - SPREADING * carried)
    for k, a in enumerate((h, e, n)):
        out_surface[k] = a[ROWS : 2 * ROWS, 0:COLS]

    for way in (N, S_):

        @pl.when(there[way])
        def _(way=way):
            for c in row_copies(way):
                c.wait_send()
            depth_message(way).wait_send()

    for way in range(8):

        @pl.when(there[way])
        def _(way=way):
            message(way).wait_send()


def deliver(t, s, surface, out_t, out_s, height, east, north, sem):
    copies = []
    for src, dst in ((t, out_t), (s, out_s)):
        copies += [(src.at[j], dst.at[:, j, :]) for j in range(ROWS)]
    copies += [(surface.at[k], dst) for k, dst in enumerate((height, east, north))]
    copies = [pltpu.make_async_copy(a, b, sem.at[i]) for i, (a, b) in enumerate(copies)]
    for c in copies:
        c.start()
    for c in copies:
        c.wait()


def solution(mesh):
    nlon, nlat = mesh.shape["lon"], mesh.shape["lat"]
    f32, bf16 = jnp.float32, jnp.bfloat16
    rows = jax.ShapeDtypeStruct((ROWS, LEVELS, COLS), f32)
    block = jax.ShapeDtypeStruct((LEVELS, ROWS, COLS), f32)
    plane = jax.ShapeDtypeStruct((ROWS, COLS), f32)
    anywhere, vmem = pl.BlockSpec(memory_space=pl.ANY), pl.BlockSpec(memory_space=pltpu.VMEM)
    dma = pltpu.SemaphoreType.DMA

    def local(*args):
        args = [pltpu.with_memory_space_constraint(a, pltpu.HBM) for a in (*args[:-1], args[-1].T)]
        columns = pl.pallas_call(
            functools.partial(exchange, nlon, nlat),
            out_shape=(rows, rows, jax.ShapeDtypeStruct((3, ROWS, COLS), f32)),
            in_specs=[anywhere] * 10,
            out_specs=(vmem,) * 3,
            scratch_shapes=[
                pltpu.VMEM((4, ROWS + 2, LEVELS, COLS), f32),
                pltpu.VMEM((2, ROWS, LEVELS, COLS), f32),
                pltpu.VMEM((FIELDS, 3 * ROWS, COLS), f32),
                pltpu.VMEM((ROWS, COLS), jnp.int32),
                pltpu.VMEM((2 * LEVELS, HID), bf16),
                pltpu.VMEM((HID, 2 * LEVELS), bf16),
                pltpu.VMEM((LEVELS, HID), bf16),
                pltpu.VMEM((ROWS + 2, 8, COLS), f32),
                pltpu.VMEM((ROWS, 8, COLS), f32),
                pltpu.VMEM((2, 24, TILE), f32),
                pltpu.VMEM((2, 24, TILE), f32),
                pltpu.VMEM((4, 8, TILE), f32),
                dma((10,)),
                dma((6,)),
                dma((2,)),
                dma((2,)),
                dma((2,)),
                dma((8,)),
                dma((8,)),
                pltpu.SemaphoreType.REGULAR,
                pltpu.SemaphoreType.REGULAR,
                pltpu.SemaphoreType.REGULAR,
            ],
            compiler_params=pltpu.CompilerParams(
                collective_id=0, has_side_effects=True, vmem_limit_bytes=LIMIT
            ),
        )(*args)
        return pl.pallas_call(
            deliver,
            out_shape=(block, block, plane, plane, plane),
            in_specs=[vmem] * 3,
            out_specs=(anywhere,) * 5,
            scratch_shapes=[dma((2 * ROWS + 3,))],
            compiler_params=pltpu.CompilerParams(vmem_limit_bytes=LIMIT),
        )(*columns)

    split, flat = P(None, "lat", "lon"), P("lat", "lon")
    return jax.shard_map(
        local,
        mesh=mesh,
        in_specs=(split,) * 4 + (flat,) * 4 + (P(), P()),
        out_specs=(split, split, flat, flat, flat),
        check_vma=False,
    )
```

```python
import functools

import jax
import jax.numpy as jnp
from jax import lax
from jax.experimental import pallas as pl
from jax.experimental.pallas import tpu as pltpu
from jax.sharding import PartitionSpec as P

MESH = pl.DeviceIdType.MESH
SUBSTEPS = 4
ADVECT = 0.1 * 0.25
SMOOTHING = 0.1
GRAVITY = 0.3 * 0.5
SPREADING = 0.3 * 0.5
BUOYANCY = 0.5 * 0.5
THERMAL = 0.2
HALINE = 0.15
MIXING_MAX = 0.45
LIMIT = 40 * 2**20
PERIOD = 16
LEVELS, ROWS, COLS, HID = 64, 8, 256, 256
GROUPS = LEVELS // 8
TILE = 128
U, T, S, V = range(4)
HEIGHT, EAST, NORTH, BUOYANT, DEPTH = range(5)
FIELDS = 5
E, W, N, S_, NE, SE, NW, SW, E_SURFACE, W_SURFACE = range(10)


def turn(x, shift, axis):
    size = x.shape[axis]
    return pltpu.roll(x, shift % size if isinstance(shift, int) else lax.rem(shift, size), axis)


def lanes_of(shape):
    return lax.broadcasted_iota(jnp.int32, shape, 1)


def levels_of(cols):
    return lax.broadcasted_iota(jnp.int32, (LEVELS, cols), 0).astype(jnp.float32)


def tall(block):
    return jnp.concatenate([block] * GROUPS, 0)


def network(w1_t, w2_t, thermal, saline):
    entries = jnp.concatenate([thermal, saline], 0).astype(jnp.bfloat16)
    hidden = jnp.tanh(jnp.dot(w1_t, entries, preferred_element_type=jnp.float32))
    return jnp.dot(
        w2_t, hidden.astype(jnp.bfloat16), preferred_element_type=jnp.float32
    )


def mixing(logits):
    return (0.5 * MIXING_MAX) * (1.0 + jnp.tanh(0.5 * logits))


def settle(tracer, kappa):
    flux = kappa * (turn(tracer, -1, 0) - tracer)
    return tracer + flux - turn(flux, 1, 0)


def face(lower, upper, speed, shared):
    return jnp.where(
        shared, ADVECT * speed * (lower + upper) - SMOOTHING * (upper - lower), 0.0
    )


def packed(vreg_of, slots, lane, rows):
    where = lanes_of((8, TILE))
    halves = []
    for r in range(2):
        total = None
        for g in range(4):
            part = None
            for a in range(slots):
                for j in rows:
                    target = 32 * g + 8 * a + j
                    moved = turn(vreg_of(a, j, 2 * g + r), target - lane + TILE, 1)
                    base = jnp.zeros_like(moved) if part is None else part
                    part = jnp.where(where == target, moved, base)
            total = part if total is None else total + part
        halves.append(total)
    return jnp.concatenate(halves, 0)


def unfolded(folded):
    return jnp.concatenate([turn(folded, -32 * g, 1) for g in range(4)], 0)


def edge_flux(lower, upper):
    first = lanes_of(lower.shape) % 32 < 8
    total, both = lower + upper, lower * upper
    speed = jnp.where(first, turn(total, -16, 1), turn(total, -8, 1))
    shared = jnp.where(first, turn(both, -24, 1), turn(both, -16, 1))
    return shared * (ADVECT * speed * total - SMOOTHING * (upper - lower))


def exchange(
    nlon, nlat,
    t, s, u, v, depth, height, east, north, w1, w2,
    out_t, out_s, out_surface,
    x, side, surface, depth_int, w1_in, w1_t, w2_t, deep, deep_east, lon_out, lon_in, corner_in,
    load_sem, row_send, row_recv, depth_send, depth_recv, send_sem, recv_sem, seam_sem, seam_corner_sem, ready_sem, east_sem, origin_sem,
):
    lon, lat = lax.axis_index("lon"), lax.axis_index("lat")
    z = lax.rem(lon, PERIOD)
    early, late, before = z == 0, z == PERIOD - 1, z == PERIOD - 2
    has_n, has_s = lat < nlat - 1, lat > 0
    sides = has_n.astype(jnp.int32) + has_s.astype(jnp.int32)
    to_east, to_west = lax.rem(lon + 1, nlon), lax.rem(lon + nlon - 1, nlon)
    device = {
        E: {"lon": to_east},
        W: {"lon": to_west},
        N: {"lat": lat + 1},
        S_: {"lat": lat - 1},
        NE: {"lon": to_east, "lat": lat + 1},
        SE: {"lon": to_east, "lat": lat - 1},
        NW: {"lon": to_west, "lat": lat + 1},
        SW: {"lon": to_west, "lat": lat - 1},
        E_SURFACE: {"lon": to_east},
        W_SURFACE: {"lon": to_west},
    }
    there = {E: True, W: True, N: has_n, NE: has_n, NW: has_n, S_: has_s, SE: has_s, SW: has_s, E_SURFACE: True, W_SURFACE: True}

    def signal(sem, way, also=True):
        @pl.when(jnp.logical_and(there[way], also))
        def _():
            pl.semaphore_signal(sem, inc=1, device_id=device[way], device_id_type=MESH)

    local = pltpu.make_async_copy
    plane = pl.ds(ROWS, ROWS)
    depth_load = local(depth, depth_int, load_sem.at[0])
    surface_loads = [
        local(f, surface.at[k, plane], load_sem.at[1 + k])
        for k, f in enumerate((height, east, north))
    ]

    def load_half(half, fields, sem):
        cut = pl.ds(half * TILE, TILE)
        for k, f in fields:
            for j in range(ROWS):
                local(f.at[:, j, cut], x.at[k, j + 1, :, cut], load_sem.at[sem]).start()

    def wait_half(half, k, count, sem):
        whole = x.at[pl.ds(k, count), pl.ds(1, ROWS), :, pl.ds(half * TILE, TILE)]
        local(whole, whole, load_sem.at[sem]).wait()

    barrier = pltpu.get_barrier_semaphore()

    @pl.when(late)
    def _():
        pl.semaphore_wait(barrier, 1 + sides)

    signal(seam_corner_sem, SE, late)
    signal(seam_corner_sem, NE, late)
    signal(seam_sem, E, late)

    for c in (depth_load, *surface_loads):
        c.start()
    load_half(1, ((T, t), (S, s)), 4)
    load_half(1, ((U, u),), 5)

    usual = jnp.logical_not(late)
    both = jnp.logical_and
    inner = both(usual, jnp.logical_not(before))
    origin = both(lon == 0, lat == 0)
    not_origin = jnp.logical_not(origin)
    at_n, at_e, at_ne = both(lon == 0, lat == 1), both(lon == 1, lat == 0), both(lon == 1, lat == 1)
    held = {S_: at_n, W: at_e, W_SURFACE: at_e, SW: at_ne}

    def free(way, also):
        return both(also, jnp.logical_not(held[way])) if way in held else also

    for way, also in ((E, inner), (NE, inner), (N, usual)):
        signal(barrier, way, both(also, not_origin))
    signal(barrier, SE, inner)
    signal(barrier, S_, usual)
    edge_of_z = jnp.logical_or(early, late)
    signal(barrier, W, jnp.logical_or(edge_of_z, at_e))
    signal(barrier, NW, edge_of_z)
    signal(barrier, SW, jnp.logical_or(edge_of_z, at_ne))
    expected = jnp.where(early, sides, jnp.where(before, 2 + 3 * sides, 1 + 2 * sides))
    beside_origin = jnp.logical_or(at_n, jnp.logical_or(at_e, at_ne))
    expected = expected + jnp.where(origin, 2, 0) - jnp.where(beside_origin, 1, 0)

    @pl.when(usual)
    def _():
        pl.semaphore_wait(barrier, expected)

    for way in (N, E, NE):
        signal(origin_sem, way, origin)
    signal(ready_sem, E, before)
    for way in (W, NW, SW):
        signal(east_sem, way, free(way, jnp.logical_not(edge_of_z)))

    remote = pltpu.make_async_remote_copy

    def row_copies(way):
        source, target = (ROWS - 1, 0) if way == N else (0, ROWS + 1)
        k = way - N
        return [
            remote(f.at[:, source, :], x.at[a, target], row_send.at[3 * k + i], row_recv.at[1 - k],
                   device_id=device[way], device_id_type=MESH)
            for i, (a, f) in enumerate(((T, t), (S, s), (V, v)))
        ]

    opposite = {E: W, W: E, N: S_, S_: N, NE: SW, SW: NE, NW: SE, SE: NW, E_SURFACE: W_SURFACE, W_SURFACE: E_SURFACE}
    lon_slot = {E: 0, W: 1, E_SURFACE: 0, W_SURFACE: 1}
    eastward, westward = (E, NE, SE, E_SURFACE), (W, NW, SW, W_SURFACE)
    corner_slot = {NE: 0, SE: 1, NW: 2, SW: 3}
    surface_rows = {N: pl.ds(2 * ROWS, ROWS), S_: pl.ds(0, ROWS)}
    tail = pl.ds(16, 8)

    def message(way):
        if way in lon_slot:
            part = pl.ds(0, 16) if way in (E, W) else tail
            src, dst = lon_out.at[lon_slot[way], part], lon_in.at[lon_slot[opposite[way]], part]
        elif way in corner_slot:
            src = lon_out.at[0 if way in (NE, SE) else 1, tail]
            dst = corner_in.at[corner_slot[opposite[way]]]
        else:
            most = pl.ds(0, FIELDS - 1)
            src, dst = surface.at[most, plane], surface.at[most, surface_rows[opposite[way]]]
        return remote(src, dst, send_sem.at[way], recv_sem.at[opposite[way]],
                      device_id=device[way], device_id_type=MESH)

    def depth_message(way):
        k = way - N
        return remote(surface.at[DEPTH, plane], surface.at[DEPTH, surface_rows[opposite[way]]],
                      depth_send.at[k], depth_recv.at[1 - k], device_id=device[way], device_id_type=MESH)

    def send_depth(also):
        for way in (N, S_):

            @pl.when(jnp.logical_and(there[way], free(way, also)))
            def _(way=way):
                depth_message(way).start()

    def send(way, also):
        @pl.when(jnp.logical_and(there[way], free(way, also)))
        def _():
            message(way).start()

    def send_rows(also):
        for way in (N, S_):

            @pl.when(jnp.logical_and(there[way], free(way, also)))
            def _(way=way):
                for c in row_copies(way):
                    c.start()

    send_rows(usual)

    @pl.when(jnp.logical_not(has_s))
    def _():
        x[:, 0] = jnp.zeros((4, LEVELS, COLS), jnp.float32)
        surface[:, 0:ROWS] = jnp.zeros((FIELDS, ROWS, COLS), jnp.float32)
        corner_in[1] = jnp.zeros((8, TILE), jnp.float32)
        corner_in[3] = jnp.zeros((8, TILE), jnp.float32)

    @pl.when(jnp.logical_not(has_n))
    def _():
        x[:, ROWS + 1] = jnp.zeros((4, LEVELS, COLS), jnp.float32)
        surface[:, 2 * ROWS : 3 * ROWS] = jnp.zeros((FIELDS, ROWS, COLS), jnp.float32)
        corner_in[0] = jnp.zeros((8, TILE), jnp.float32)
        corner_in[2] = jnp.zeros((8, TILE), jnp.float32)

    depth_load.wait()
    deeps = depth_int[...].astype(jnp.float32)
    surface[DEPTH, plane] = deeps
    beside = jnp.where(lanes_of((ROWS, COLS)) == COLS - 1, 0.0, turn(deeps, -1, 1))
    beside = jnp.minimum(deeps, beside)
    for j in range(ROWS):
        deep[j + 1] = jnp.broadcast_to(deeps[j : j + 1], (8, COLS))
        deep_east[j] = jnp.broadcast_to(beside[j : j + 1], (8, COLS))

    def pack_half(half):
        cut = pl.ds(half * TILE, TILE)
        edge = TILE - 1 if half else 0
        level = lax.broadcasted_iota(jnp.int32, (8, TILE), 0).astype(jnp.float32)
        where = lanes_of((8, TILE))

        def wet(j, q):
            return level + 8.0 * q < deep[j + 1, :, cut]

        def vreg(a, j, q):
            if a == 3:
                return jnp.where(wet(j, q), 1.0, 0.0)
            return x[(T, S, U)[a], j + 1, pl.ds(8 * q, 8), cut]

        def surface_part():
            for j in range(ROWS):
                total = jnp.zeros((8, TILE), jnp.float32)
                for q in range(GROUPS):
                    rows = pl.ds(8 * q, 8)
                    density = THERMAL * x[T, j + 1, rows, cut] - HALINE * x[S, j + 1, rows, cut]
                    total = total + jnp.where(wet(j, q), density, 0.0)
                surface[BUOYANT, ROWS + j : ROWS + j + 1, cut] = (LEVELS**-0.5) * jnp.sum(total, 0, keepdims=True)
            kept = (where >= TILE - 8) if half else (where < 8)
            lon_out[1 - half, 16:24] = sum(
                turn(jnp.where(kept, surface[f, plane, cut], 0.0), 16 * f, 1)
                for f in range(FIELDS)
            )

        def tracer_part():
            lon_out[1 - half, 0:16] = packed(vreg, 4, edge, range(ROWS))

        return surface_part, tracer_part

    surface_part, tracer_part = pack_half(1)
    wait_half(1, T, 2, 4)
    for c in surface_loads:
        c.wait()
    at_once = jnp.logical_not(inner)
    place = lax.rem(lat, 4)

    def surface_first(also):
        @pl.when(also)
        def _():
            surface_part()
            for way in (NE, SE, E_SURFACE):
                send(way, at_once)

    surface_first(place == 2)
    wait_half(1, U, 1, 5)
    tracer_part()
    send(E, at_once)
    surface_first(place != 2)
    load_half(0, ((T, t), (S, s), (U, u)), 6)
    for j in range(ROWS):
        local(v.at[:, j, :], x.at[V, j + 1], load_sem.at[7]).start()
    weights = [local(w1, w1_in, load_sem.at[8]), local(w2, w2_t, load_sem.at[9])]
    for c in weights:
        c.start()
    send_depth(usual)
    wait_half(0, U, 3, 6)
    for part in pack_half(0):
        part()
    middle = jnp.logical_and(usual, jnp.logical_not(early))
    for way in westward:
        send(way, middle)
    near_north = lax.rem(lat, 2) == 0
    far_north = jnp.logical_not(near_north)

    @pl.when(late)
    def _():
        pl.semaphore_wait(ready_sem, 1)

    send_rows(late)
    send_depth(late)
    for way in westward:
        send(way, late)
    send(N, near_north)
    send(S_, far_north)

    def send_east(also):
        @pl.when(both(also, not_origin))
        def _():
            pl.semaphore_wait(east_sem, 1 + sides)

        for way in eastward:
            send(way, also)

    send_east(early)

    for c in weights:
        c.wait()
    w1_t[...] = w1_in[...].astype(jnp.float32).T.astype(jnp.bfloat16)
    all_v = x.at[V, pl.ds(1, ROWS)]
    local(all_v, all_v, load_sem.at[7]).wait()

    def row(j):
        level = levels_of(COLS)
        speed = x[U, j + 1]
        speed = speed + turn(speed, -1, 1)
        here, above, below = deep[j + 1], deep[j + 2], deep[j]
        open_east = level < tall(deep_east[j])
        open_north = level < tall(jnp.minimum(here, above))
        open_south = level < tall(jnp.minimum(here, below))
        wet = level < tall(here)
        wet_below = level + 1.0 < tall(here)
        speed_north = x[V, j + 1] + x[V, j + 2]
        speed_south = x[V, j + 1] + x[V, j]

        def lateral(k):
            own = x[k, j + 1]
            flux = face(own, turn(own, -1, 1), speed, open_east)
            return own - (
                flux
                - turn(flux, 1, 1)
                + face(own, x[k, j + 2], speed_north, open_north)
                - face(x[k, j], own, speed_south, open_south)
            )

        thermal, saline = lateral(T), lateral(S)
        side[0, j] = thermal
        side[1, j] = saline
        logits = network(
            w1_t[...], w2_t[...], jnp.where(wet, thermal, 0.0), jnp.where(wet, saline, 0.0)
        )
        kappa = jnp.where(wet_below, mixing(logits), 0.0)
        out_t[j] = settle(thermal, kappa)
        out_s[j] = settle(saline, kappa)

    pl.loop(1, ROWS - 1)(row)

    send_east(both(inner, jnp.logical_not(early)))
    send(N, far_north)
    send(S_, near_north)

    @pl.when(beside_origin)
    def _():
        pl.semaphore_wait(origin_sem, 1)

    @pl.when(at_n)
    def _():
        for c in row_copies(S_):
            c.start()
        depth_message(S_).start()
        message(S_).start()

    @pl.when(at_e)
    def _():
        message(W).start()
        message(W_SURFACE).start()

    @pl.when(at_ne)
    def _():
        message(SW).start()

    def side_pack(half, rows):
        cut = pl.ds(half * TILE, TILE)
        return packed(
            lambda a, j, q: side[a, j, pl.ds(8 * q, 8), cut],
            2,
            TILE - 1 if half else 0,
            rows,
        )

    inside = range(1, ROWS - 1)
    part_east, part_west = side_pack(1, inside), side_pack(0, inside)


    def outer(north):
        for way in (N, S_):

            @pl.when(jnp.logical_and(there[way], north if way == N else jnp.logical_not(north)))
            def _(way=way):
                k = way - N
                rows = x.at[pl.ds(T, 3), ROWS + 1 if way == N else 0]
                local(rows, rows, row_recv.at[k]).wait()
                depth_message(opposite[way]).wait_recv()

        edge = jnp.where(north, ROWS - 1, 0)
        beyond = jnp.where(north, 2 * ROWS, ROWS - 1)
        deep[jnp.where(north, ROWS + 1, 0)] = jnp.broadcast_to(surface[DEPTH, pl.ds(beyond, 1)], (8, COLS))
        row(edge)
        return side_pack(1, [edge]), side_pack(0, [edge])

    near_east, near_west = outer(near_north)
    far_east, far_west = outer(far_north)
    part_east = part_east + near_east + far_east
    part_west = part_west + near_west + far_west

    @pl.when(early)
    def _():
        pl.semaphore_wait(seam_sem, 1)

    send(W, early)
    send(W_SURFACE, early)

    @pl.when(early)
    def _():
        pl.semaphore_wait(seam_corner_sem, sides)

    send(NW, early)
    send(SW, early)

    for way in (E, W):
        message(opposite[way]).wait_recv()

    own_east, own_west = lon_out[0, 0:16], lon_out[1, 0:16]
    from_east, from_west = lon_in[0, 0:16], lon_in[1, 0:16]
    at_east = part_east - edge_flux(own_east, from_east)
    at_west = part_west + edge_flux(from_west, own_west)
    lane16 = lanes_of((16, TILE))
    first_slot = lane16 % 32 < 8
    thermal = unfolded(jnp.where(first_slot, at_west, turn(at_east, 8, 1)))
    saline = unfolded(jnp.where(first_slot, turn(at_west, -8, 1), at_east))
    wet = unfolded(jnp.where(first_slot, turn(own_west, -24, 1), turn(own_east, -16, 1)))
    lane = lanes_of((LEVELS, TILE))
    wet = jnp.where(lane < 16, wet, 0.0)
    wet_below = jnp.where(levels_of(TILE) < LEVELS - 1.0, turn(wet, -1, 0), 0.0)
    logits = network(w1_t[...], w2_t[...], thermal * wet, saline * wet)
    kappa = mixing(logits) * wet * wet_below
    for out, tracer in ((out_t, thermal), (out_s, saline)):
        new = settle(tracer, kappa)
        for j in range(ROWS):
            out[j, :, 0:TILE] = jnp.where(lane == 0, turn(new, -j, 1), out[j, :, 0:TILE])
            out[j, :, TILE:] = jnp.where(lane == TILE - 1, turn(new, TILE - 1 - 8 - j, 1), out[j, :, TILE:])

    for way in (N, S_):

        @pl.when(there[way])
        def _(way=way):
            for c in row_copies(way):
                c.wait_send()
            depth_message(way).wait_send()

    for way in range(10):

        @pl.when(there[way])
        def _(way=way):
            message(way).wait_send()

    for way in (N, S_, NE, SE, NW, SW, E_SURFACE, W_SURFACE):

        @pl.when(there[way])
        def _(way=way):
            message(opposite[way]).wait_recv()

    third = jnp.concatenate(
        [
            corner_in[1] + corner_in[3],
            lon_in[0, 16:24] + lon_in[1, 16:24],
            corner_in[0] + corner_in[2],
        ],
        0,
    )
    where = lanes_of((3 * ROWS, TILE))
    around = jnp.logical_or(where < 8, where >= TILE - 8)
    field = [
        jnp.concatenate([surface[f], jnp.where(around, turn(third, -16 * f, 1), 0.0)], 1)
        for f in range(FIELDS)
    ]
    h, e, n, b, d = field
    def ahead_behind(a, axis, by):
        return turn(a, -by, axis), turn(a, by, axis)

    def current(flow, axis):
        flows, depths = ahead_behind(flow, axis, 1), ahead_behind(d, axis, 1)
        after, before_ = ahead_behind(b, axis, 2)
        forces = -BUOYANCY * (after - b), -BUOYANCY * (b - before_)
        return [
            (f, g, p <= 0.0, p * (1.0 / LEVELS)) for f, g, p in zip(flows, forces, depths)
        ]

    land = d <= 0.0
    state = {1: current(e, 1), 0: current(n, 0)}
    for step in range(SUBSTEPS):
        carried = 0.0
        if step == SUBSTEPS - 1:
            (e, force, _, _), (n, force_n, _, _) = state[1][0], state[0][0]
            e, n = turn(e, 1, 1), turn(n, 1, 0)
            rises = [ahead_behind(h, axis, 1) for axis in (1, 0)]
            e = e - GRAVITY * (rises[0][0] - rises[0][1]) + turn(force, 1, 1)
            n = n - GRAVITY * (rises[1][0] - rises[1][1]) + turn(force_n, 1, 0)
            e, n = jnp.where(land, 0.0, e), jnp.where(land, 0.0, n)
        for axis in (1, 0):
            after, before_ = ahead_behind(h, axis, 2)
            slopes = after - h, h - before_
            state[axis] = [
                (jnp.where(dry, 0.0, f - GRAVITY * slope + g), g, dry, c)
                for (f, g, dry, c), slope in zip(state[axis], slopes)
            ]
            (ahead, _, _, c_ahead), (behind, _, _, c_behind) = state[axis]
            carried = carried + (c_ahead * ahead - c_behind * behind)
        h = jnp.where(land, 0.0, h - SPREADING * carried)
    for k, a in enumerate((h, e, n)):
        out_surface[k] = a[ROWS : 2 * ROWS, 0:COLS]


def deliver(t, s, surface, out_t, out_s, height, east, north, sem):
    copies = []
    for src, dst in ((t, out_t), (s, out_s)):
        copies += [(src.at[j], dst.at[:, j, :]) for j in range(ROWS)]
    copies += [(surface.at[k], dst) for k, dst in enumerate((height, east, north))]
    copies = [pltpu.make_async_copy(a, b, sem.at[i]) for i, (a, b) in enumerate(copies)]
    for c in copies:
        c.start()
    for c in copies:
        c.wait()


def solution(mesh):
    nlon, nlat = mesh.shape["lon"], mesh.shape["lat"]
    f32, bf16 = jnp.float32, jnp.bfloat16
    rows = jax.ShapeDtypeStruct((ROWS, LEVELS, COLS), f32)
    block = jax.ShapeDtypeStruct((LEVELS, ROWS, COLS), f32)
    plane = jax.ShapeDtypeStruct((ROWS, COLS), f32)
    anywhere, vmem = pl.BlockSpec(memory_space=pl.ANY), pl.BlockSpec(memory_space=pltpu.VMEM)
    dma = pltpu.SemaphoreType.DMA

    def local(*args):
        args = [pltpu.with_memory_space_constraint(a, pltpu.HBM) for a in (*args[:-1], args[-1].T)]
        columns = pl.pallas_call(
            functools.partial(exchange, nlon, nlat),
            out_shape=(rows, rows, jax.ShapeDtypeStruct((3, ROWS, COLS), f32)),
            in_specs=[anywhere] * 10,
            out_specs=(vmem,) * 3,
            scratch_shapes=[
                pltpu.VMEM((4, ROWS + 2, LEVELS, COLS), f32),
                pltpu.VMEM((2, ROWS, LEVELS, COLS), f32),
                pltpu.VMEM((FIELDS, 3 * ROWS, COLS), f32),
                pltpu.VMEM((ROWS, COLS), jnp.int32),
                pltpu.VMEM((2 * LEVELS, HID), bf16),
                pltpu.VMEM((HID, 2 * LEVELS), bf16),
                pltpu.VMEM((LEVELS, HID), bf16),
                pltpu.VMEM((ROWS + 2, 8, COLS), f32),
                pltpu.VMEM((ROWS, 8, COLS), f32),
                pltpu.VMEM((2, 24, TILE), f32),
                pltpu.VMEM((2, 24, TILE), f32),
                pltpu.VMEM((4, 8, TILE), f32),
                dma((10,)),
                dma((6,)),
                dma((2,)),
                dma((2,)),
                dma((2,)),
                dma((10,)),
                dma((10,)),
                pltpu.SemaphoreType.REGULAR,
                pltpu.SemaphoreType.REGULAR,
                pltpu.SemaphoreType.REGULAR,
                pltpu.SemaphoreType.REGULAR,
                pltpu.SemaphoreType.REGULAR,
            ],
            compiler_params=pltpu.CompilerParams(
                collective_id=0, has_side_effects=True, vmem_limit_bytes=LIMIT
            ),
        )(*args)
        return pl.pallas_call(
            deliver,
            out_shape=(block, block, plane, plane, plane),
            in_specs=[vmem] * 3,
            out_specs=(anywhere,) * 5,
            scratch_shapes=[dma((2 * ROWS + 3,))],
            compiler_params=pltpu.CompilerParams(vmem_limit_bytes=LIMIT),
        )(*columns)

    split, flat = P(None, "lat", "lon"), P("lat", "lon")
    return jax.shard_map(
        local,
        mesh=mesh,
        in_specs=(split,) * 4 + (flat,) * 4 + (P(), P()),
        out_specs=(split, split, flat, flat, flat),
        check_vma=False,
    )
```

```python
import functools

import jax
import jax.numpy as jnp
from jax import lax
from jax.experimental import pallas as pl
from jax.experimental.pallas import tpu as pltpu
from jax.sharding import PartitionSpec as P

MESH = pl.DeviceIdType.MESH
SUBSTEPS = 4
ADVECT = 0.1 * 0.25
SMOOTHING = 0.1
GRAVITY = 0.3 * 0.5
SPREADING = 0.3 * 0.5
BUOYANCY = 0.5 * 0.5
THERMAL = 0.2
HALINE = 0.15
MIXING_MAX = 0.45
LIMIT = 40 * 2**20
PERIOD = 16
LEVELS, ROWS, COLS, HID = 64, 8, 256, 256
GROUPS = LEVELS // 8
TILE = 128
U, T, S, V = range(4)
HEIGHT, EAST, NORTH, BUOYANT, DEPTH = range(5)
FIELDS = 5
E, W, N, S_, NE, SE, NW, SW, E_SURFACE, W_SURFACE = range(10)


def turn(x, shift, axis):
    size = x.shape[axis]
    return pltpu.roll(x, shift % size if isinstance(shift, int) else lax.rem(shift, size), axis)


def lanes_of(shape):
    return lax.broadcasted_iota(jnp.int32, shape, 1)


def levels_of(cols):
    return lax.broadcasted_iota(jnp.int32, (LEVELS, cols), 0).astype(jnp.float32)


def tall(block):
    return jnp.concatenate([block] * GROUPS, 0)


def network(w1_t, w2_t, thermal, saline):
    entries = jnp.concatenate([thermal, saline], 0).astype(jnp.bfloat16)
    hidden = jnp.tanh(jnp.dot(w1_t, entries, preferred_element_type=jnp.float32))
    return jnp.dot(
        w2_t, hidden.astype(jnp.bfloat16), preferred_element_type=jnp.float32
    )


def mixing(logits):
    return (0.5 * MIXING_MAX) * (1.0 + jnp.tanh(0.5 * logits))


def settle(tracer, kappa):
    flux = kappa * (turn(tracer, -1, 0) - tracer)
    return tracer + flux - turn(flux, 1, 0)


def face(lower, upper, speed, shared):
    return jnp.where(
        shared, ADVECT * speed * (lower + upper) - SMOOTHING * (upper - lower), 0.0
    )


def packed(vreg_of, slots, lane, rows):
    where = lanes_of((8, TILE))
    halves = []
    for r in range(2):
        total = None
        for g in range(4):
            part = None
            for a in range(slots):
                for j in rows:
                    target = 32 * g + 8 * a + j
                    moved = turn(vreg_of(a, j, 2 * g + r), target - lane + TILE, 1)
                    base = jnp.zeros_like(moved) if part is None else part
                    part = jnp.where(where == target, moved, base)
            total = part if total is None else total + part
        halves.append(total)
    return jnp.concatenate(halves, 0)


def unfolded(folded):
    return jnp.concatenate([turn(folded, -32 * g, 1) for g in range(4)], 0)


def edge_flux(lower, upper):
    first = lanes_of(lower.shape) % 32 < 8
    total, both = lower + upper, lower * upper
    speed = jnp.where(first, turn(total, -16, 1), turn(total, -8, 1))
    shared = jnp.where(first, turn(both, -24, 1), turn(both, -16, 1))
    return shared * (ADVECT * speed * total - SMOOTHING * (upper - lower))


def exchange(
    nlon, nlat,
    t, s, u, v, depth, height, east, north, w1, w2,
    out_t, out_s, out_surface,
    x, side, surface, depth_int, w1_in, w1_t, w2_t, deep, deep_east, lon_out, lon_in, corner_in,
    load_sem, row_send, row_recv, depth_send, depth_recv, send_sem, recv_sem, seam_sem, seam_corner_sem, ready_sem, east_sem, origin_sem,
):
    lon, lat = lax.axis_index("lon"), lax.axis_index("lat")
    z = lax.rem(lon, PERIOD)
    early, late, before = z == 0, z == PERIOD - 1, z == PERIOD - 2
    has_n, has_s = lat < nlat - 1, lat > 0
    sides = has_n.astype(jnp.int32) + has_s.astype(jnp.int32)
    to_east, to_west = lax.rem(lon + 1, nlon), lax.rem(lon + nlon - 1, nlon)
    device = {
        E: {"lon": to_east},
        W: {"lon": to_west},
        N: {"lat": lat + 1},
        S_: {"lat": lat - 1},
        NE: {"lon": to_east, "lat": lat + 1},
        SE: {"lon": to_east, "lat": lat - 1},
        NW: {"lon": to_west, "lat": lat + 1},
        SW: {"lon": to_west, "lat": lat - 1},
        E_SURFACE: {"lon": to_east},
        W_SURFACE: {"lon": to_west},
    }
    there = {E: True, W: True, N: has_n, NE: has_n, NW: has_n, S_: has_s, SE: has_s, SW: has_s, E_SURFACE: True, W_SURFACE: True}

    def signal(sem, way, also=True):
        @pl.when(jnp.logical_and(there[way], also))
        def _():
            pl.semaphore_signal(sem, inc=1, device_id=device[way], device_id_type=MESH)

    local = pltpu.make_async_copy
    plane = pl.ds(ROWS, ROWS)
    depth_load = local(depth, depth_int, load_sem.at[0])
    surface_loads = [
        local(f, surface.at[k, plane], load_sem.at[1 + k])
        for k, f in enumerate((height, east, north))
    ]

    def load_half(half, fields, sem):
        cut = pl.ds(half * TILE, TILE)
        for k, f in fields:
            for j in range(ROWS):
                local(f.at[:, j, cut], x.at[k, j + 1, :, cut], load_sem.at[sem]).start()

    def wait_half(half, k, count, sem):
        whole = x.at[pl.ds(k, count), pl.ds(1, ROWS), :, pl.ds(half * TILE, TILE)]
        local(whole, whole, load_sem.at[sem]).wait()

    barrier = pltpu.get_barrier_semaphore()

    @pl.when(late)
    def _():
        pl.semaphore_wait(barrier, 1 + sides)

    signal(seam_corner_sem, SE, late)
    signal(seam_corner_sem, NE, late)
    signal(seam_sem, E, late)

    load_half(1, ((T, t), (S, s)), 4)
    for c in (depth_load, *surface_loads):
        c.start()
    load_half(1, ((U, u),), 5)

    usual = jnp.logical_not(late)
    both = jnp.logical_and
    inner = both(usual, jnp.logical_not(before))
    origin = both(lon == 0, lat == 0)
    not_origin = jnp.logical_not(origin)
    at_n, at_e, at_ne = both(lon == 0, lat == 1), both(lon == 1, lat == 0), both(lon == 1, lat == 1)
    held = {S_: at_n, W: at_e, W_SURFACE: at_e, SW: at_ne}

    def free(way, also):
        return both(also, jnp.logical_not(held[way])) if way in held else also

    for way, also in ((E, inner), (NE, inner), (N, usual)):
        signal(barrier, way, both(also, not_origin))
    signal(barrier, SE, inner)
    signal(barrier, S_, usual)
    edge_of_z = jnp.logical_or(early, late)
    signal(barrier, W, jnp.logical_or(edge_of_z, at_e))
    signal(barrier, NW, edge_of_z)
    signal(barrier, SW, jnp.logical_or(edge_of_z, at_ne))
    expected = jnp.where(early, sides, jnp.where(before, 2 + 3 * sides, 1 + 2 * sides))
    beside_origin = jnp.logical_or(at_n, jnp.logical_or(at_e, at_ne))
    expected = expected + jnp.where(origin, 2, 0) - jnp.where(beside_origin, 1, 0)

    @pl.when(usual)
    def _():
        pl.semaphore_wait(barrier, expected)

    for way in (N, E, NE):
        signal(origin_sem, way, origin)
    signal(ready_sem, E, before)
    for way in (W, NW, SW):
        signal(east_sem, way, free(way, jnp.logical_not(edge_of_z)))

    remote = pltpu.make_async_remote_copy

    def row_copies(way):
        source, target = (ROWS - 1, 0) if way == N else (0, ROWS + 1)
        k = way - N
        return [
            remote(f.at[:, source, :], x.at[a, target], row_send.at[3 * k + i], row_recv.at[1 - k],
                   device_id=device[way], device_id_type=MESH)
            for i, (a, f) in enumerate(((T, t), (S, s), (V, v)))
        ]

    opposite = {E: W, W: E, N: S_, S_: N, NE: SW, SW: NE, NW: SE, SE: NW, E_SURFACE: W_SURFACE, W_SURFACE: E_SURFACE}
    lon_slot = {E: 0, W: 1, E_SURFACE: 0, W_SURFACE: 1}
    eastward, westward = (E, NE, SE, E_SURFACE), (W, NW, SW, W_SURFACE)
    corner_slot = {NE: 0, SE: 1, NW: 2, SW: 3}
    surface_rows = {N: pl.ds(2 * ROWS, ROWS), S_: pl.ds(0, ROWS)}
    tail = pl.ds(16, 8)

    def message(way):
        if way in lon_slot:
            part = pl.ds(0, 16) if way in (E, W) else tail
            src, dst = lon_out.at[lon_slot[way], part], lon_in.at[lon_slot[opposite[way]], part]
        elif way in corner_slot:
            src = lon_out.at[0 if way in (NE, SE) else 1, tail]
            dst = corner_in.at[corner_slot[opposite[way]]]
        else:
            most = pl.ds(0, FIELDS - 1)
            src, dst = surface.at[most, plane], surface.at[most, surface_rows[opposite[way]]]
        return remote(src, dst, send_sem.at[way], recv_sem.at[opposite[way]],
                      device_id=device[way], device_id_type=MESH)

    def depth_message(way):
        k = way - N
        return remote(surface.at[DEPTH, plane], surface.at[DEPTH, surface_rows[opposite[way]]],
                      depth_send.at[k], depth_recv.at[1 - k], device_id=device[way], device_id_type=MESH)

    def send_depth(also):
        for way in (N, S_):

            @pl.when(jnp.logical_and(there[way], free(way, also)))
            def _(way=way):
                depth_message(way).start()

    def send(way, also):
        @pl.when(jnp.logical_and(there[way], free(way, also)))
        def _():
            message(way).start()

    def send_rows(also):
        for way in (N, S_):

            @pl.when(jnp.logical_and(there[way], free(way, also)))
            def _(way=way):
                for c in row_copies(way):
                    c.start()

    send_rows(usual)

    @pl.when(jnp.logical_not(has_s))
    def _():
        x[:, 0] = jnp.zeros((4, LEVELS, COLS), jnp.float32)
        surface[:, 0:ROWS] = jnp.zeros((FIELDS, ROWS, COLS), jnp.float32)
        corner_in[1] = jnp.zeros((8, TILE), jnp.float32)
        corner_in[3] = jnp.zeros((8, TILE), jnp.float32)

    @pl.when(jnp.logical_not(has_n))
    def _():
        x[:, ROWS + 1] = jnp.zeros((4, LEVELS, COLS), jnp.float32)
        surface[:, 2 * ROWS : 3 * ROWS] = jnp.zeros((FIELDS, ROWS, COLS), jnp.float32)
        corner_in[0] = jnp.zeros((8, TILE), jnp.float32)
        corner_in[2] = jnp.zeros((8, TILE), jnp.float32)

    depth_load.wait()
    deeps = depth_int[...].astype(jnp.float32)
    surface[DEPTH, plane] = deeps
    beside = jnp.where(lanes_of((ROWS, COLS)) == COLS - 1, 0.0, turn(deeps, -1, 1))
    beside = jnp.minimum(deeps, beside)
    for j in range(ROWS):
        deep[j + 1] = jnp.broadcast_to(deeps[j : j + 1], (8, COLS))
        deep_east[j] = jnp.broadcast_to(beside[j : j + 1], (8, COLS))

    def pack_half(half):
        cut = pl.ds(half * TILE, TILE)
        edge = TILE - 1 if half else 0
        level = lax.broadcasted_iota(jnp.int32, (8, TILE), 0).astype(jnp.float32)
        where = lanes_of((8, TILE))

        def wet(j, q):
            return level + 8.0 * q < deep[j + 1, :, cut]

        def vreg(a, j, q):
            if a == 3:
                return jnp.where(wet(j, q), 1.0, 0.0)
            return x[(T, S, U)[a], j + 1, pl.ds(8 * q, 8), cut]

        def surface_part():
            for j in range(ROWS):
                total = jnp.zeros((8, TILE), jnp.float32)
                for q in range(GROUPS):
                    rows = pl.ds(8 * q, 8)
                    density = THERMAL * x[T, j + 1, rows, cut] - HALINE * x[S, j + 1, rows, cut]
                    total = total + jnp.where(wet(j, q), density, 0.0)
                surface[BUOYANT, ROWS + j : ROWS + j + 1, cut] = (LEVELS**-0.5) * jnp.sum(total, 0, keepdims=True)
            kept = (where >= TILE - 8) if half else (where < 8)
            lon_out[1 - half, 16:24] = sum(
                turn(jnp.where(kept, surface[f, plane, cut], 0.0), 16 * f, 1)
                for f in range(FIELDS)
            )

        def tracer_part():
            lon_out[1 - half, 0:16] = packed(vreg, 4, edge, range(ROWS))

        return surface_part, tracer_part

    surface_part, tracer_part = pack_half(1)
    wait_half(1, T, 2, 4)
    for c in surface_loads:
        c.wait()
    at_once = jnp.logical_not(inner)
    place = lax.rem(lat, 4)

    def surface_first(also):
        @pl.when(also)
        def _():
            surface_part()
            for way in (SE, NE, E_SURFACE):
                send(way, at_once)

    surface_first(place == 2)
    wait_half(1, U, 1, 5)
    tracer_part()
    send(E, at_once)
    surface_first(place != 2)
    load_half(0, ((T, t), (S, s), (U, u)), 6)
    for j in range(ROWS):
        local(v.at[:, j, :], x.at[V, j + 1], load_sem.at[7]).start()
    weights = [local(w1, w1_in, load_sem.at[8]), local(w2, w2_t, load_sem.at[9])]
    for c in weights:
        c.start()
    send_depth(usual)
    wait_half(0, U, 3, 6)
    for part in pack_half(0):
        part()
    middle = jnp.logical_and(usual, jnp.logical_not(early))
    for way in westward:
        send(way, middle)
    near_north = lax.rem(lat, 2) == 0
    far_north = jnp.logical_not(near_north)

    @pl.when(late)
    def _():
        pl.semaphore_wait(ready_sem, 1)

    send_rows(late)
    send_depth(late)
    for way in westward:
        send(way, late)
    send(N, near_north)
    send(S_, far_north)

    def send_east(also):
        @pl.when(both(also, not_origin))
        def _():
            pl.semaphore_wait(east_sem, 1 + sides)

        for way in eastward:
            send(way, also)

    send_east(early)

    for c in weights:
        c.wait()
    w1_t[...] = w1_in[...].astype(jnp.float32).T.astype(jnp.bfloat16)
    all_v = x.at[V, pl.ds(1, ROWS)]
    local(all_v, all_v, load_sem.at[7]).wait()

    def row(j):
        level = levels_of(COLS)
        speed = x[U, j + 1]
        speed = speed + turn(speed, -1, 1)
        here, above, below = deep[j + 1], deep[j + 2], deep[j]
        open_east = level < tall(deep_east[j])
        open_north = level < tall(jnp.minimum(here, above))
        open_south = level < tall(jnp.minimum(here, below))
        wet = level < tall(here)
        wet_below = level + 1.0 < tall(here)
        speed_north = x[V, j + 1] + x[V, j + 2]
        speed_south = x[V, j + 1] + x[V, j]

        def lateral(k):
            own = x[k, j + 1]
            flux = face(own, turn(own, -1, 1), speed, open_east)
            return own - (
                flux
                - turn(flux, 1, 1)
                + face(own, x[k, j + 2], speed_north, open_north)
                - face(x[k, j], own, speed_south, open_south)
            )

        thermal, saline = lateral(T), lateral(S)
        side[0, j] = thermal
        side[1, j] = saline
        logits = network(
            w1_t[...], w2_t[...], jnp.where(wet, thermal, 0.0), jnp.where(wet, saline, 0.0)
        )
        kappa = jnp.where(wet_below, mixing(logits), 0.0)
        out_t[j] = settle(thermal, kappa)
        out_s[j] = settle(saline, kappa)

    pl.loop(1, ROWS - 1)(row)

    send_east(both(inner, jnp.logical_not(early)))
    send(N, far_north)
    send(S_, near_north)

    @pl.when(beside_origin)
    def _():
        pl.semaphore_wait(origin_sem, 1)

    @pl.when(at_n)
    def _():
        for c in row_copies(S_):
            c.start()
        depth_message(S_).start()
        message(S_).start()

    @pl.when(at_e)
    def _():
        message(W).start()
        message(W_SURFACE).start()

    @pl.when(at_ne)
    def _():
        message(SW).start()

    def side_pack(half, rows):
        cut = pl.ds(half * TILE, TILE)
        return packed(
            lambda a, j, q: side[a, j, pl.ds(8 * q, 8), cut],
            2,
            TILE - 1 if half else 0,
            rows,
        )

    inside = range(1, ROWS - 1)
    part_east, part_west = side_pack(1, inside), side_pack(0, inside)


    def outer(north):
        for way in (N, S_):

            @pl.when(jnp.logical_and(there[way], north if way == N else jnp.logical_not(north)))
            def _(way=way):
                k = way - N
                rows = x.at[pl.ds(T, 3), ROWS + 1 if way == N else 0]
                local(rows, rows, row_recv.at[k]).wait()
                depth_message(opposite[way]).wait_recv()

        edge = jnp.where(north, ROWS - 1, 0)
        beyond = jnp.where(north, 2 * ROWS, ROWS - 1)
        deep[jnp.where(north, ROWS + 1, 0)] = jnp.broadcast_to(surface[DEPTH, pl.ds(beyond, 1)], (8, COLS))
        row(edge)
        return side_pack(1, [edge]), side_pack(0, [edge])

    near_east, near_west = outer(near_north)
    far_east, far_west = outer(far_north)
    part_east = part_east + near_east + far_east
    part_west = part_west + near_west + far_west

    @pl.when(early)
    def _():
        pl.semaphore_wait(seam_sem, 1)

    send(W, early)
    send(W_SURFACE, early)

    @pl.when(early)
    def _():
        pl.semaphore_wait(seam_corner_sem, sides)

    send(NW, early)
    send(SW, early)

    for way in (E, W):
        message(opposite[way]).wait_recv()

    own_east, own_west = lon_out[0, 0:16], lon_out[1, 0:16]
    from_east, from_west = lon_in[0, 0:16], lon_in[1, 0:16]
    at_east = part_east - edge_flux(own_east, from_east)
    at_west = part_west + edge_flux(from_west, own_west)
    lane16 = lanes_of((16, TILE))
    first_slot = lane16 % 32 < 8
    thermal = unfolded(jnp.where(first_slot, at_west, turn(at_east, 8, 1)))
    saline = unfolded(jnp.where(first_slot, turn(at_west, -8, 1), at_east))
    wet = unfolded(jnp.where(first_slot, turn(own_west, -24, 1), turn(own_east, -16, 1)))
    lane = lanes_of((LEVELS, TILE))
    wet = jnp.where(lane < 16, wet, 0.0)
    wet_below = jnp.where(levels_of(TILE) < LEVELS - 1.0, turn(wet, -1, 0), 0.0)
    logits = network(w1_t[...], w2_t[...], thermal * wet, saline * wet)
    kappa = mixing(logits) * wet * wet_below
    for out, tracer in ((out_t, thermal), (out_s, saline)):
        new = settle(tracer, kappa)
        for j in range(ROWS):
            out[j, :, 0:TILE] = jnp.where(lane == 0, turn(new, -j, 1), out[j, :, 0:TILE])
            out[j, :, TILE:] = jnp.where(lane == TILE - 1, turn(new, TILE - 1 - 8 - j, 1), out[j, :, TILE:])

    for way in (N, S_):

        @pl.when(there[way])
        def _(way=way):
            for c in row_copies(way):
                c.wait_send()
            depth_message(way).wait_send()

    for way in range(10):

        @pl.when(there[way])
        def _(way=way):
            message(way).wait_send()

    for way in (N, S_, NE, SE, NW, SW, E_SURFACE, W_SURFACE):

        @pl.when(there[way])
        def _(way=way):
            message(opposite[way]).wait_recv()

    third = jnp.concatenate(
        [
            corner_in[1] + corner_in[3],
            lon_in[0, 16:24] + lon_in[1, 16:24],
            corner_in[0] + corner_in[2],
        ],
        0,
    )
    where = lanes_of((3 * ROWS, TILE))
    around = jnp.logical_or(where < 8, where >= TILE - 8)
    field = [
        jnp.concatenate([surface[f], jnp.where(around, turn(third, -16 * f, 1), 0.0)], 1)
        for f in range(FIELDS)
    ]
    h, e, n, b, d = field
    def ahead_behind(a, axis, by):
        return turn(a, -by, axis), turn(a, by, axis)

    def current(flow, axis):
        flows, depths = ahead_behind(flow, axis, 1), ahead_behind(d, axis, 1)
        after, before_ = ahead_behind(b, axis, 2)
        forces = -BUOYANCY * (after - b), -BUOYANCY * (b - before_)
        return [
            (f, g, p <= 0.0, p * (1.0 / LEVELS)) for f, g, p in zip(flows, forces, depths)
        ]

    land = d <= 0.0
    state = {1: current(e, 1), 0: current(n, 0)}
    for step in range(SUBSTEPS):
        carried = 0.0
        if step == SUBSTEPS - 1:
            (e, force, _, _), (n, force_n, _, _) = state[1][0], state[0][0]
            e, n = turn(e, 1, 1), turn(n, 1, 0)
            rises = [ahead_behind(h, axis, 1) for axis in (1, 0)]
            e = e - GRAVITY * (rises[0][0] - rises[0][1]) + turn(force, 1, 1)
            n = n - GRAVITY * (rises[1][0] - rises[1][1]) + turn(force_n, 1, 0)
            e, n = jnp.where(land, 0.0, e), jnp.where(land, 0.0, n)
        for axis in (1, 0):
            after, before_ = ahead_behind(h, axis, 2)
            slopes = after - h, h - before_
            state[axis] = [
                (jnp.where(dry, 0.0, f - GRAVITY * slope + g), g, dry, c)
                for (f, g, dry, c), slope in zip(state[axis], slopes)
            ]
            (ahead, _, _, c_ahead), (behind, _, _, c_behind) = state[axis]
            carried = carried + (c_ahead * ahead - c_behind * behind)
        h = jnp.where(land, 0.0, h - SPREADING * carried)
    for k, a in enumerate((h, e, n)):
        out_surface[k] = a[ROWS : 2 * ROWS, 0:COLS]


def deliver(t, s, surface, out_t, out_s, height, east, north, sem):
    copies = []
    for src, dst in ((t, out_t), (s, out_s)):
        copies += [(src.at[j], dst.at[:, j, :]) for j in range(ROWS)]
    copies += [(surface.at[k], dst) for k, dst in enumerate((height, east, north))]
    copies = [pltpu.make_async_copy(a, b, sem.at[i]) for i, (a, b) in enumerate(copies)]
    for c in copies:
        c.start()
    for c in copies:
        c.wait()


def solution(mesh):
    nlon, nlat = mesh.shape["lon"], mesh.shape["lat"]
    f32, bf16 = jnp.float32, jnp.bfloat16
    rows = jax.ShapeDtypeStruct((ROWS, LEVELS, COLS), f32)
    block = jax.ShapeDtypeStruct((LEVELS, ROWS, COLS), f32)
    plane = jax.ShapeDtypeStruct((ROWS, COLS), f32)
    anywhere, vmem = pl.BlockSpec(memory_space=pl.ANY), pl.BlockSpec(memory_space=pltpu.VMEM)
    dma = pltpu.SemaphoreType.DMA

    def local(*args):
        args = [pltpu.with_memory_space_constraint(a, pltpu.HBM) for a in (*args[:-1], args[-1].T)]
        columns = pl.pallas_call(
            functools.partial(exchange, nlon, nlat),
            out_shape=(rows, rows, jax.ShapeDtypeStruct((3, ROWS, COLS), f32)),
            in_specs=[anywhere] * 10,
            out_specs=(vmem,) * 3,
            scratch_shapes=[
                pltpu.VMEM((4, ROWS + 2, LEVELS, COLS), f32),
                pltpu.VMEM((2, ROWS, LEVELS, COLS), f32),
                pltpu.VMEM((FIELDS, 3 * ROWS, COLS), f32),
                pltpu.VMEM((ROWS, COLS), jnp.int32),
                pltpu.VMEM((2 * LEVELS, HID), bf16),
                pltpu.VMEM((HID, 2 * LEVELS), bf16),
                pltpu.VMEM((LEVELS, HID), bf16),
                pltpu.VMEM((ROWS + 2, 8, COLS), f32),
                pltpu.VMEM((ROWS, 8, COLS), f32),
                pltpu.VMEM((2, 24, TILE), f32),
                pltpu.VMEM((2, 24, TILE), f32),
                pltpu.VMEM((4, 8, TILE), f32),
                dma((10,)),
                dma((6,)),
                dma((2,)),
                dma((2,)),
                dma((2,)),
                dma((10,)),
                dma((10,)),
                pltpu.SemaphoreType.REGULAR,
                pltpu.SemaphoreType.REGULAR,
                pltpu.SemaphoreType.REGULAR,
                pltpu.SemaphoreType.REGULAR,
                pltpu.SemaphoreType.REGULAR,
            ],
            compiler_params=pltpu.CompilerParams(
                collective_id=0, has_side_effects=True, vmem_limit_bytes=LIMIT
            ),
        )(*args)
        return pl.pallas_call(
            deliver,
            out_shape=(block, block, plane, plane, plane),
            in_specs=[vmem] * 3,
            out_specs=(anywhere,) * 5,
            scratch_shapes=[dma((2 * ROWS + 3,))],
            compiler_params=pltpu.CompilerParams(vmem_limit_bytes=LIMIT),
        )(*columns)

    split, flat = P(None, "lat", "lon"), P("lat", "lon")
    return jax.shard_map(
        local,
        mesh=mesh,
        in_specs=(split,) * 4 + (flat,) * 4 + (P(), P()),
        out_specs=(split, split, flat, flat, flat),
        check_vma=False,
    )
```
